128 devices in a mesh: depth: 16 (over x, y), tile: 8 (over z, core).
Axes of the slice: x: 4, y: 4, z: 4, core: 2. Of those that a mesh axis runs over, the one named last changes fastest.
Arguments:
- measured: float32 [64, 2048, 1024], P('depth', 'tile'), may hold values from 0.1 to 3
- estimate: float32 [64, 2048, 1024], P('depth', 'tile'), may hold values from 0.5 to 2
- extinction: float32 [64, 2048, 1024], P('depth', 'tile'), may hold values from 0.002 to 0.05
- psf_rows: float32 [16, 65], replicated, may hold values from 0.05 to 1
- psf_cols: float32 [16, 65], replicated, may hold values from 0.05 to 1
- stratum: int32 [64], P('depth'), may hold values from 0 to 15
- seam_flags: int32 [7], replicated, may hold values 0 or 1
Outputs:
- updated: float32 [64, 2048, 1024], P('depth', 'tile')
- projection: float32 [2048, 1024], P('tile')
The draws below stay inside these ranges and needn't reach their ends.
All inputs are finite; a program needn't handle non-finite values.
Results may differ from the reference program's by a relative error of at most 0.000073.
Values sent between devices are 32-bit elements; how exact they have to be, the bound alone decides.
No kernel may reach another device: no remote copies, remote signals or barrier semaphores. Data moves between devices by JAX's collectives and lax.ppermute only.
A program may use at most 128 MiB of HBM per device.

```python
import math
import jax
import jax.numpy as jnp
from jax import lax

ROWS_DEV = 256
NX = 1024
HALF = 32
TAPS = 65
STRATA = 16
NZ = 64
NY = 2048
N_TILE = 8


def touch_ends(array, key, smallest, high):
    spot = [jax.random.randint(jax.random.fold_in(key, axis), (), 0, length) for axis, length in enumerate(array.shape)]
    widest = array.shape.index(max(array.shape))
    beside = spot[:widest] + [(spot[widest] + 1) % array.shape[widest]] + spot[widest + 1:]
    return array.at[tuple(spot)].set(smallest).at[tuple(beside)].set(high)


def block_levels(stream_key, extent, shards, low, high):
    def one(axis_at, shards_of):
        heights = jax.random.uniform(jax.random.fold_in(jax.random.fold_in(stream_key, 6), axis_at), (shards_of,), jnp.float32, low / len(shards), high / len(shards))
        return jnp.repeat(jnp.exp(heights), extent[axis_at] // shards_of).reshape((-1,) + (1,) * (len(extent) - axis_at - 1))

    gain = one(*shards[0])
    for cut in shards[1:]:
        gain = gain * one(*cut)
    return gain


def setup_inputs(seed: int = 0) -> dict:
    keys = jax.random.split(jax.random.key(seed), 8)
    measured = jnp.clip(jnp.exp(math.log(3.0) - 3.4011974 * jax.random.uniform(keys[0], (NZ, NY, NX), jnp.float32) ** block_levels(keys[0], (NZ, NY, NX), ((0, 16), (1, 8)), -0.2, 0.2)), 0.1, 3.0)
    estimate = jnp.clip(0.5 + 1.5 * jax.random.uniform(keys[1], (NZ, NY, NX), jnp.float32) ** block_levels(keys[1], (NZ, NY, NX), ((0, 16), (1, 8)), -0.2, 0.2), 0.5, 2.0)
    extinction = jnp.clip(jnp.exp(math.log(0.05) - 3.218876 * jax.random.uniform(keys[2], (NZ, NY, NX), jnp.float32) ** block_levels(keys[2], (NZ, NY, NX), ((0, 16), (1, 8)), -0.2, 0.2)), 0.002, 0.05)
    psf_rows = jnp.clip(jnp.exp(jax.random.uniform(keys[3], (STRATA, TAPS), jnp.float32, math.log(0.05), math.log(1.0))), 0.05, 1.0)
    psf_cols = jnp.clip(jnp.exp(jax.random.uniform(keys[4], (STRATA, TAPS), jnp.float32, math.log(0.05), math.log(1.0))), 0.05, 1.0)
    stratum = touch_ends(jax.random.randint(keys[5], (NZ,), 0, STRATA), jax.random.fold_in(keys[5], 1), 0, STRATA - 1).astype(jnp.int32)
    seam_flags = touch_ends((jax.random.randint(keys[6], (N_TILE - 1,), 0, 4) < 3).astype(jnp.int32), jax.random.fold_in(keys[6], 1), 0, 1)
    return {"measured": measured, "estimate": estimate, "extinction": extinction, "psf_rows": psf_rows, "psf_cols": psf_cols, "stratum": stratum, "seam_flags": seam_flags}


def banded(kernel, row_count, col_count, offset):
    length = kernel.shape[0]
    offsets = jnp.arange(col_count, dtype=jnp.int32)[None, :] - jnp.arange(row_count, dtype=jnp.int32)[:, None] + offset
    inside = (offsets >= 0) & (offsets < length)
    picked = kernel[jnp.clip(offsets, 0, length - 1).astype(jnp.int32)]
    return jnp.where(inside, picked, jnp.zeros_like(picked))


def reference(measured, estimate, extinction, psf_rows, psf_cols, stratum, seam_flags):
    optical = jnp.cumsum(extinction, axis=0) - extinction
    weighted = jnp.exp(-optical) * estimate
    vertical = psf_rows / jnp.sum(psf_rows, axis=1, keepdims=True)
    lateral = psf_cols / jnp.sum(psf_cols, axis=1, keepdims=True)
    segment = jnp.concatenate([jnp.zeros((1,), jnp.int32), jnp.cumsum(1 - seam_flags).astype(jnp.int32)])
    row_segment = segment[(jnp.arange(NY, dtype=jnp.int32) // ROWS_DEV).astype(jnp.int32)]
    joined = row_segment[:, None] == row_segment[None, :]
    highest = lax.Precision.HIGHEST

    def one_plane(inputs):
        plane_weighted, plane_measured, plane_estimate, index = inputs
        band_rows = banded(vertical[index], NY, NY, HALF)
        band_rows = jnp.where(joined, band_rows, jnp.zeros_like(band_rows))
        band_cols = banded(lateral[index], NX, NX, HALF)
        blurred = jnp.dot(jnp.dot(band_rows, plane_weighted, precision=highest), band_cols.T, precision=highest)
        quotient = plane_measured / blurred
        spread = jnp.dot(jnp.dot(band_rows.T, quotient, precision=highest), band_cols, precision=highest)
        return plane_estimate * spread

    updated = lax.map(one_plane, (weighted, measured, estimate, stratum))
    return updated, jnp.max(updated, axis=0)
```

```python
import functools

import jax
import jax.numpy as jnp
from jax import lax
from jax.experimental import pallas as pl
from jax.experimental.pallas import tpu as pltpu
from jax.sharding import PartitionSpec as P

SIDE = 4
HALF = 32
TAPS = 65
BF = jnp.bfloat16
F32 = jnp.float32
VMEM_LIMIT = 56 * 1024 * 1024


def params(**kw):
    return pltpu.CompilerParams(vmem_limit_bytes=VMEM_LIMIT, **kw)


def whole():
    return pl.BlockSpec(memory_space=pltpu.VMEM)


def smem():
    return pl.BlockSpec(memory_space=pltpu.SMEM)


def place():
    depth = lax.axis_index("depth")
    tile = lax.axis_index("tile")
    x, y, core = depth // SIDE, depth % SIDE, tile % 2
    first = jnp.where(core == 0, y, x)
    second = jnp.where(core == 0, x, y)
    return first, second, core, tile


def turn(value, k):
    return lax.rem(value + (k + 2 * SIDE), SIDE)


def perm(stage, k, tiles):
    pairs = []
    for x in range(SIDE):
        for y in range(SIDE):
            for tile in range(tiles):
                along_y = (tile % 2 == 0) == (stage == 0)
                tx, ty = (x, (y + k) % SIDE) if along_y else ((x + k) % SIDE, y)
                pairs.append(((x * SIDE + y) * tiles + tile, (tx * SIDE + ty) * tiles + tile))
    return pairs


def exchange(stage, sign, parts):
    tiles = lax.axis_size("tile")
    got = [parts[0]] + [None] * (SIDE - 1)
    for k in (2, 1, 3):
        got[k] = lax.ppermute(parts[k], ("depth", "tile"), perm(stage, sign * k, tiles))
    return got


def split(value):
    high = value.astype(BF)
    return high, (value - high.astype(F32)).astype(BF)


def rows_at(index, size):
    return pl.ds(pl.multiple_of(index * size, size), size)


def sums_kernel(ext, est_top, est_bot, mea_top, mea_bot, up, down, o0, o1, o2, o3, acc):
    plane = pl.program_id(0)
    first, _, _, _ = place()
    rim = 2 * HALF
    rows = acc.shape[0]

    @pl.when(plane == 0)
    def _():
        acc[...] = jnp.zeros_like(acc)

    up[0, :rim] = jnp.exp(-acc[:rim]) * est_top[0]
    down[0, :rim] = jnp.exp(-acc[rows - rim :]) * est_bot[0]
    up[0, rim:] = mea_top[0]
    down[0, rim:] = mea_bot[0]
    acc[...] += ext[0]

    @pl.when(plane == pl.num_programs(0) - 1)
    def _():
        for k, out in enumerate((o0, o1, o2, o3)):
            out[...] = acc[rows_at(turn(first, k), rows // SIDE)]


def sums(extinction, estimate, measured):
    planes, rows, cols = extinction.shape
    rim, quarter = 2 * HALF, rows // SIDE
    last = rows // rim - 1
    plane_block = pl.BlockSpec((1, rim + HALF, cols), lambda p: (p, 0, 0))
    part = pl.BlockSpec((quarter, cols), lambda p: (0, 0))
    return pl.pallas_call(
        sums_kernel,
        grid=(planes,),
        in_specs=[
            pl.BlockSpec((1, rows, cols), lambda p: (p, 0, 0)),
            pl.BlockSpec((1, rim, cols), lambda p: (p, 0, 0)),
            pl.BlockSpec((1, rim, cols), lambda p: (p, last, 0)),
            pl.BlockSpec((1, HALF, cols), lambda p: (p, 0, 0)),
            pl.BlockSpec((1, HALF, cols), lambda p: (p, rows // HALF - 1, 0)),
        ],
        out_specs=[plane_block, plane_block] + [part] * SIDE,
        out_shape=[jax.ShapeDtypeStruct((planes, rim + HALF, cols), F32)] * 2
        + [jax.ShapeDtypeStruct((quarter, cols), F32)] * SIDE,
        scratch_shapes=[pltpu.VMEM((rows, cols), F32)],
        compiler_params=params(),
    )(extinction, estimate, estimate, measured, measured)


def local(kernel, shapes, args, scratch=(), specs=None):
    out = [jax.ShapeDtypeStruct(s, F32) for s in shapes]
    return pl.pallas_call(
        kernel,
        in_specs=specs or [whole()] * len(args),
        out_specs=[whole()] * len(out),
        out_shape=out,
        scratch_shapes=list(scratch),
        compiler_params=params(),
    )(*args)


def regroup_kernel(r0, r1, r2, r3, b0, b1, b2, b3):
    first, second, _, _ = place()
    rows = r0.shape[0] // SIDE
    for j, source in enumerate((r0, r1, r2, r3)):
        for k, out in enumerate((b0, b1, b2, b3)):
            out[turn(first, -j)] = source[rows_at(turn(second, k), rows)]


def scan_kernel(c0, c1, c2, c3, d0, d1, d2, d3, buf):
    _, second, core, _ = place()

    def slot(j, k):
        g = turn(second, -k)
        return jnp.where(core == 0, g * SIDE + j, j * SIDE + g)

    for k, source in enumerate((c0, c1, c2, c3)):
        for j in range(SIDE):
            buf[slot(j, k)] = source[j]
    total = jnp.zeros(buf.shape[1:], F32)
    for d in range(SIDE * SIDE):
        value = buf[d]
        buf[d] = total
        total = total + value
    for k, out in enumerate((d0, d1, d2, d3)):
        for j in range(SIDE):
            out[j] = buf[slot(j, k)]


def ungroup_kernel(e0, e1, e2, e3, h0, h1, h2, h3):
    first, second, _, _ = place()
    rows = e0.shape[1]
    for m, source in enumerate((e0, e1, e2, e3)):
        for k, out in enumerate((h0, h1, h2, h3)):
            out[rows_at(turn(second, m), rows)] = source[turn(first, -k)]


def place_kernel(sign, i0, i1, i2, i3, out):
    first, _, _, _ = place()
    rows = i0.shape[0]
    for k, source in enumerate((i0, i1, i2, i3)):
        out[rows_at(turn(first, sign * k), rows)] = source[...]


def above_of(parts):
    quarter, cols = parts[0].shape
    small = quarter // SIDE
    got = exchange(0, 1, parts)
    packed = local(regroup_kernel, [(SIDE, small, cols)] * SIDE, got)
    got = exchange(1, 1, packed)
    scanned = local(
        scan_kernel,
        [(SIDE, small, cols)] * SIDE,
        got,
        [pltpu.VMEM((SIDE * SIDE, small, cols), F32)],
    )
    got = exchange(1, -1, scanned)
    back = local(ungroup_kernel, [(quarter, cols)] * SIDE, got)
    got = exchange(0, -1, back)
    return local(functools.partial(place_kernel, 1), [(quarter * SIDE, cols)], got)[0]


def max_split_kernel(r0, r1, r2, r3, b0, b1, b2, b3):
    _, second, _, _ = place()
    rows = r0.shape[0] // SIDE
    for k, out in enumerate((b0, b1, b2, b3)):
        at = rows_at(turn(second, k), rows)
        out[...] = jnp.maximum(jnp.maximum(r0[at], r1[at]), jnp.maximum(r2[at], r3[at]))


def max_kernel(r0, r1, r2, r3, out):
    out[...] = jnp.maximum(jnp.maximum(r0[...], r1[...]), jnp.maximum(r2[...], r3[...]))


def join_kernel(stage, i0, i1, i2, i3, out):
    first, second, _, _ = place()
    rows = i0.shape[0]
    for k, source in enumerate((i0, i1, i2, i3)):
        out[rows_at(turn(second if stage else first, -k), rows)] = source[...]


def highest(parts):
    quarter, cols = parts[0].shape
    small = quarter // SIDE
    got = exchange(0, 1, parts)
    packed = local(max_split_kernel, [(small, cols)] * SIDE, got)
    got = exchange(1, 1, packed)
    top = local(max_kernel, [(small, cols)], got)[0]
    got = exchange(1, 1, [top] * SIDE)
    joined = local(functools.partial(join_kernel, 1), [(quarter, cols)], got)[0]
    got = exchange(0, 1, [joined] * SIDE)
    return local(functools.partial(join_kernel, 0), [(quarter * SIDE, cols)], got)[0]


def bands_kernel(stratum, taps, v_ref, l_ref):
    def toeplitz(row, count, shift):
        line = taps[0, row : row + 1]
        line = line / jnp.sum(line, axis=1, keepdims=True)
        wide = jnp.broadcast_to(line, (count, line.shape[1]))
        return pltpu.roll(wide, shift, 1, stride=1, stride_axis=0)

    for way in range(2):
        band = toeplitz(way, v_ref.shape[3], 0)
        v_ref[0, way, 0], v_ref[0, way, 1] = split(band)
        ring = toeplitz(3 - way, 256, 256 - HALF)
        k = lax.broadcasted_iota(jnp.int32, ring.shape, 0)
        n = lax.broadcasted_iota(jnp.int32, ring.shape, 1)
        zero = jnp.zeros_like(ring)
        main = jnp.where(jnp.abs(n - k) <= HALF, ring, zero)
        left = jnp.where(k - n > HALF, ring, zero)[128:]
        right = jnp.where(n - k > HALF, ring, zero)[:128]
        for at, part in ((0, left), (128, main), (384, right)):
            high, low = split(part)
            l_ref[0, way, 0, at : at + part.shape[0]] = high
            l_ref[0, way, 1, at : at + part.shape[0]] = low


def bands(psf_rows, psf_cols, stratum):
    planes = stratum.shape[0]
    taps = jnp.stack([psf_rows, psf_rows[:, ::-1], psf_cols, psf_cols[:, ::-1]], axis=1)
    taps = jnp.pad(taps, ((0, 0), (0, 0), (0, 256 - TAPS)))
    return pl.pallas_call(
        bands_kernel,
        grid_spec=pltpu.PrefetchScalarGridSpec(
            num_scalar_prefetch=1,
            grid=(planes,),
            in_specs=[pl.BlockSpec((1, 4, 256), lambda p, s: (s[p], 0, 0))],
            out_specs=[
                pl.BlockSpec((1, 2, 2, 192, 256), lambda p, s: (p, 0, 0, 0, 0)),
                pl.BlockSpec((1, 2, 2, 512, 256), lambda p, s: (p, 0, 0, 0, 0)),
            ],
        ),
        out_shape=[
            jax.ShapeDtypeStruct((planes, 2, 2, 192, 256), BF),
            jax.ShapeDtypeStruct((planes, 2, 2, 512, 256), BF),
        ],
        compiler_params=params(),
    )(stratum, taps)


def dot(a, b):
    return jnp.dot(a, b, preferred_element_type=F32)


def dot3(a_high, a_low, b_high, b_low):
    return dot(a_high, b_high) + (dot(a_high, b_low) + dot(a_low, b_high))


def step_kernel(
    seams, ext, est, mea, above, above_top, above_bot, rim_top, rim_bot, v_ref, l_ref,
    upd, o0, o1, o2, o3, optical, top, wh, wl, mh, ml, qh, ql, nh, nl,
):
    plane = pl.program_id(0)
    first, _, _, tile = place()
    rows, cols = optical.shape
    rim = 2 * HALF
    ends = lax.axis_size("tile") - 1
    join_top = jnp.where(tile > 0, seams[jnp.maximum(tile - 1, 0)], 0) == 1
    join_bot = jnp.where(tile < ends, seams[jnp.minimum(tile, ends - 1)], 0) == 1

    @pl.when(plane == 0)
    def _():
        optical[...] = above[...]
        for ref in (mh, ml, nh, nl):
            edge = jnp.zeros((ref.shape[0], 128), BF)
            ref[:, :128] = edge
            ref[:, ref.shape[1] - 128 :] = edge

    for joined, far, packed, at in (
        (join_top, above_top, rim_top, 0),
        (join_bot, above_bot, rim_bot, rows + rim),
    ):
        value = jnp.where(joined, jnp.exp(-far[...]) * packed[0, :rim], 0.0)
        wh[at : at + rim], wl[at : at + rim] = split(value)
    for r in range(0, rows, 64):
        depth = optical[r : r + 64]
        value = jnp.exp(-depth) * est[0, r : r + 64]
        wh[rim + r : rim + r + 64], wl[rim + r : rim + r + 64] = split(value)
        optical[r : r + 64] = depth + ext[0, r : r + 64]

    def vertical(way, sh, sl, dh, dl):
        total = dh.shape[0]
        for at in range(0, total, 192):
            m = min(192, total - at)
            depth = min(256, m + rim)
            th, tl = v_ref[0, way, 0, :m, :depth], v_ref[0, way, 1, :m, :depth]
            for c in range(0, cols, 256):
                result = dot3(th, tl, sh[at : at + depth, c : c + 256], sl[at : at + depth, c : c + 256])
                dh[at : at + m, 128 + c : 384 + c], dl[at : at + m, 128 + c : 384 + c] = split(result)

    vertical(0, wh, wl, mh, ml)
    lh, ll = l_ref.at[0, 0, 0], l_ref.at[0, 0, 1]
    for c in range(0, cols, 256):
        for a, b in ((0, 160), (160, 320)):
            blurred = dot3(mh[a:b, c : c + 512], ml[a:b, c : c + 512], lh[...], ll[...])
            s = slice(c, c + 256)
            if a == 0:
                halo = jnp.where(join_top, rim_top[0, rim:, s] / blurred[:HALF], 0.0)
                inner = mea[0, : b - HALF, s] / blurred[HALF:]
                qh[:HALF, s], ql[:HALF, s] = split(halo)
                qh[HALF:b, s], ql[HALF:b, s] = split(inner)
            else:
                halo = jnp.where(join_bot, rim_bot[0, rim:, s] / blurred[b - a - HALF :], 0.0)
                inner = mea[0, a - HALF :, s] / blurred[: b - a - HALF]
                qh[b - HALF :, s], ql[b - HALF :, s] = split(halo)
                qh[a : b - HALF, s], ql[a : b - HALF, s] = split(inner)

    vertical(1, qh, ql, nh, nl)
    lh, ll = l_ref.at[0, 1, 0], l_ref.at[0, 1, 1]
    for c in range(0, cols, 256):
        s = slice(c, c + 256)
        for a in range(0, rows, 128):
            t = slice(a, a + 128)
            spread = dot3(nh[t, c : c + 512], nl[t, c : c + 512], lh[...], ll[...])
            result = est[0, t, s] * spread
            upd[0, t, s] = result
            top[t, s] = jnp.maximum(jnp.where(plane == 0, result, top[t, s]), result)

    @pl.when(plane == pl.num_programs(0) - 1)
    def _():
        for k, out in enumerate((o0, o1, o2, o3)):
            out[...] = top[rows_at(turn(first, k), rows // SIDE)]


def step(seams, ext, est, mea, above, above_top, above_bot, rim_top, rim_bot, v, l):
    planes, rows, cols = ext.shape
    rim, quarter = 2 * HALF, rows // SIDE
    stack = pl.BlockSpec((1, rows, cols), lambda p: (p, 0, 0))
    pack = pl.BlockSpec((1, rim + HALF, cols), lambda p: (p, 0, 0))
    part = pl.BlockSpec((quarter, cols), lambda p: (0, 0))
    return pl.pallas_call(
        step_kernel,
        grid=(planes,),
        in_specs=[
            smem(), stack, stack, stack, whole(), whole(), whole(), pack, pack,
            pl.BlockSpec((1,) + v.shape[1:], lambda p: (p, 0, 0, 0, 0)),
            pl.BlockSpec((1,) + l.shape[1:], lambda p: (p, 0, 0, 0, 0)),
        ],
        out_specs=[stack] + [part] * SIDE,
        out_shape=[jax.ShapeDtypeStruct((planes, rows, cols), F32)]
        + [jax.ShapeDtypeStruct((quarter, cols), F32)] * SIDE,
        scratch_shapes=[
            pltpu.VMEM((rows, cols), F32),
            pltpu.VMEM((rows, cols), F32),
            pltpu.VMEM((rows + 2 * rim, cols), BF),
            pltpu.VMEM((rows + 2 * rim, cols), BF),
            pltpu.VMEM((rows + rim, cols + 256), BF),
            pltpu.VMEM((rows + rim, cols + 256), BF),
            pltpu.VMEM((rows + rim, cols), BF),
            pltpu.VMEM((rows + rim, cols), BF),
            pltpu.VMEM((rows, cols + 256), BF),
            pltpu.VMEM((rows, cols + 256), BF),
        ],
        compiler_params=params(),
    )(seams, ext, est, mea, above, above_top, above_bot, rim_top, rim_bot, v, l)


def on_device(measured, estimate, extinction, psf_rows, psf_cols, stratum, seam_flags):
    rows = measured.shape[1]
    rim = 2 * HALF
    tiles = lax.axis_size("tile")
    onward = [(i, i + 1) for i in range(tiles - 1)]
    backward = [(i + 1, i) for i in range(tiles - 1)]
    up, down, *parts = sums(extinction, estimate, measured)
    rim_top = lax.ppermute(down, "tile", onward)
    rim_bot = lax.ppermute(up, "tile", backward)
    v, l = bands(psf_rows, psf_cols, stratum)
    above = above_of(parts)
    above_top = lax.ppermute(above[rows - rim :], "tile", onward)
    above_bot = lax.ppermute(above[:rim], "tile", backward)
    updated, *tops = step(
        seam_flags, extinction, estimate, measured, above, above_top, above_bot, rim_top, rim_bot, v, l
    )
    return updated, highest(tops)


def solution(mesh):
    return jax.shard_map(
        on_device,
        mesh=mesh,
        in_specs=(
            P("depth", "tile", None),
            P("depth", "tile", None),
            P("depth", "tile", None),
            P(),
            P(),
            P("depth"),
            P(),
        ),
        out_specs=(P("depth", "tile", None), P("tile", None)),
        check_vma=False,
    )
```

```python
import jax
import jax.numpy as jnp
from jax import lax
from jax.experimental import pallas as pl
from jax.experimental.pallas import tpu as pltpu
from jax.sharding import PartitionSpec as P

SIDE = 4
HALF = 32
TAPS = 65
BF = jnp.bfloat16
F32 = jnp.float32


def params(mib):
    return pltpu.CompilerParams(vmem_limit_bytes=mib << 20)


def whole():
    return pl.BlockSpec(memory_space=pltpu.VMEM)


def smem():
    return pl.BlockSpec(memory_space=pltpu.SMEM)


def place():
    depth = lax.axis_index("depth")
    tile = lax.axis_index("tile")
    return depth // SIDE, depth % SIDE, tile % 2, tile


PAIRINGS = {
    (0, 0): (("y", 1), ("y", 3), ("x", 1), ("x", 3)),
    (0, 1): (("x", 1), ("x", 3), ("y", 1), ("y", 3)),
    (1, 0): (("y", 3), ("y", 1), ("x", 3), ("x", 1)),
    (1, 1): (("x", 3), ("x", 1), ("y", 3), ("y", 1)),
}


def pairs(piece, number, tiles):
    result = []
    for x in range(SIDE):
        for y in range(SIDE):
            for tile in range(tiles):
                axis, flip = PAIRINGS[(tile % 2, piece)][number]
                tx, ty = (x, y ^ flip) if axis == "y" else (x ^ flip, y)
                result.append(((x * SIDE + y) * tiles + tile, (tx * SIDE + ty) * tiles + tile))
    return result


def swap(value, piece, number):
    return lax.ppermute(value, ("depth", "tile"), pairs(piece, number, lax.axis_size("tile")))


def side(piece):
    x, y, core, _ = place()
    bits = []
    for c in range(2):
        axis, flip = PAIRINGS[(c, piece)][0]
        value = y if axis == "y" else x
        bits.append((value + 1) // 2 % 2 if flip == 1 else value // 2)
    return jnp.where(core == 0, bits[0], bits[1])


def split(value):
    high = value.astype(BF)
    return high, (value - high.astype(F32)).astype(BF)


def rows_at(index, size):
    return pl.ds(pl.multiple_of(index * size, size), size)


def sums_kernel(ext, out, buf, sems):
    block = out.shape[0] // sems.shape[0]
    copies = []
    for i in range(sems.shape[0]):
        rows = pl.ds(i * block, block)
        copies.append(pltpu.make_async_copy(ext.at[:, rows], buf.at[:, rows], sems.at[i]))
        copies[-1].start()
    for i, copy in enumerate(copies):
        copy.wait()
        rows = pl.ds(i * block, block)
        total = buf[0, rows]
        for plane in range(1, buf.shape[0]):
            total = total + buf[plane, rows]
        out[rows] = total


def sums(extinction):
    planes, rows, cols = extinction.shape
    return pl.pallas_call(
        sums_kernel,
        in_specs=[pl.BlockSpec(memory_space=pl.ANY)],
        out_specs=whole(),
        out_shape=jax.ShapeDtypeStruct((rows, cols), F32),
        scratch_shapes=[pltpu.VMEM((planes, rows, cols), F32), pltpu.SemaphoreType.DMA((8,))],
        compiler_params=params(60),
    )(extinction)


def rims_kernel(ext_top, ext_bot, est_top, est_bot, mea_top, mea_bot, up, down, acc_top, acc_bot):
    rim = 2 * HALF
    for ext, est, mea, out, acc in (
        (ext_top, est_top, mea_top, up, acc_top),
        (ext_bot, est_bot, mea_bot, down, acc_bot),
    ):

        @pl.when(pl.program_id(0) == 0)
        def _():
            acc[...] = jnp.zeros_like(acc)

        out[0, :rim] = jnp.exp(-acc[...]) * est[0]
        out[0, rim:] = mea[0]
        acc[...] += ext[0]


def rims(extinction, estimate, measured):
    planes, rows, cols = extinction.shape
    rim = 2 * HALF
    far = rows // rim - 1
    top = pl.BlockSpec((1, rim, cols), lambda p: (p, 0, 0))
    bot = pl.BlockSpec((1, rim, cols), lambda p: (p, far, 0))
    out = pl.BlockSpec((1, rim + HALF, cols), lambda p: (p, 0, 0))
    return pl.pallas_call(
        rims_kernel,
        grid=(planes,),
        in_specs=[
            top, bot, top, bot,
            pl.BlockSpec((1, HALF, cols), lambda p: (p, 0, 0)),
            pl.BlockSpec((1, HALF, cols), lambda p: (p, rows // HALF - 1, 0)),
        ],
        out_specs=[out, out],
        out_shape=[jax.ShapeDtypeStruct((planes, rim + HALF, cols), F32)] * 2,
        scratch_shapes=[pltpu.VMEM((rim, cols), F32)] * 2,
        compiler_params=params(60),
        cost_estimate=pl.CostEstimate(flops=1 << 20, bytes_accessed=8 << 20, transcendentals=1 << 19),
    )(extinction, extinction, estimate, estimate, measured, measured)


def scan_kernel(parts, out):
    running = jnp.zeros(parts.shape[1:], F32)
    for slab in range(parts.shape[0]):
        value = parts[slab]
        out[slab] = running
        running = running + value


def above_of(total, meanwhile):
    rows, cols = total.shape
    slabs = lax.axis_size("depth")
    parts = total.reshape(slabs, rows // slabs, cols)
    parts = lax.all_to_all(parts, "depth", 0, 0, tiled=True)
    prefixes = pl.pallas_call(
        scan_kernel,
        in_specs=[whole()],
        out_specs=whole(),
        out_shape=jax.ShapeDtypeStruct(parts.shape, F32),
        compiler_params=params(16),
    )(parts)
    prefixes, meanwhile = lax.optimization_barrier((prefixes, meanwhile))
    return lax.all_to_all(prefixes, "depth", 0, 0, tiled=True).reshape(rows, cols), meanwhile


def highest(parts):
    joined = []
    held = [jnp.maximum(keep, swap(give, piece, 0)) for piece, (keep, give) in enumerate(parts)]
    for number in range(1, 4):
        held = [jnp.maximum(value, swap(value, piece, number)) for piece, value in enumerate(held)]
    for piece, mine in enumerate(held):
        other = swap(mine, piece, 0)
        first = side(piece) == 0
        joined += [jnp.where(first, mine, other), jnp.where(first, other, mine)]
    return jnp.concatenate(joined)


def bands_kernel(stratum, taps, v_ref, l_ref):
    def toeplitz(row, count, shift):
        line = taps[0, row : row + 1]
        line = line / jnp.sum(line, axis=1, keepdims=True)
        wide = jnp.broadcast_to(line, (count, line.shape[1]))
        return pltpu.roll(wide, shift, 1, stride=1, stride_axis=0)

    for way in range(2):
        band = toeplitz(way, v_ref.shape[3], 0)
        v_ref[0, way, 0], v_ref[0, way, 1] = split(band)
        ring = toeplitz(3 - way, 256, 256 - HALF)
        k = lax.broadcasted_iota(jnp.int32, ring.shape, 0)
        n = lax.broadcasted_iota(jnp.int32, ring.shape, 1)
        zero = jnp.zeros_like(ring)
        main = jnp.where(jnp.abs(n - k) <= HALF, ring, zero)
        left = jnp.where(k - n > HALF, ring, zero)[128:]
        right = jnp.where(n - k > HALF, ring, zero)[:128]
        for at, part in ((0, left), (128, main), (384, right)):
            high, low = split(part)
            l_ref[0, way, 0, at : at + part.shape[0]] = high
            l_ref[0, way, 1, at : at + part.shape[0]] = low


def bands(psf_rows, psf_cols, stratum):
    planes = stratum.shape[0]
    taps = jnp.stack([psf_rows, psf_rows[:, ::-1], psf_cols, psf_cols[:, ::-1]], axis=1)
    taps = jnp.pad(taps, ((0, 0), (0, 0), (0, 256 - TAPS)))
    return pl.pallas_call(
        bands_kernel,
        grid_spec=pltpu.PrefetchScalarGridSpec(
            num_scalar_prefetch=1,
            grid=(planes,),
            in_specs=[pl.BlockSpec((1, 4, 256), lambda p, s: (s[p], 0, 0))],
            out_specs=[
                pl.BlockSpec((1, 2, 2, 192, 256), lambda p, s: (p, 0, 0, 0, 0)),
                pl.BlockSpec((1, 2, 2, 512, 256), lambda p, s: (p, 0, 0, 0, 0)),
            ],
        ),
        out_shape=[
            jax.ShapeDtypeStruct((planes, 2, 2, 192, 256), BF),
            jax.ShapeDtypeStruct((planes, 2, 2, 512, 256), BF),
        ],
        compiler_params=params(60),
        cost_estimate=pl.CostEstimate(flops=1 << 22, bytes_accessed=6 << 20, transcendentals=0),
    )(stratum, taps)


def dot(a, b):
    return jnp.dot(a, b, preferred_element_type=F32)


def dot3(a_high, a_low, b_high, b_low):
    return dot(a_high, b_high) + (dot(a_high, b_low) + dot(a_low, b_high))


def step_kernel(
    seams, ext, est, mea, above, above_top, above_bot, rim_top, rim_bot, v_ref, l_ref,
    upd, o0, o1, o2, o3, optical, top, wh, wl, mh, ml, qh, ql, nh, nl,
):
    plane = pl.program_id(0)
    _, _, _, tile = place()
    rows, cols = optical.shape
    rim = 2 * HALF
    ends = lax.axis_size("tile") - 1
    join_top = jnp.where(tile > 0, seams[jnp.maximum(tile - 1, 0)], 0) == 1
    join_bot = jnp.where(tile < ends, seams[jnp.minimum(tile, ends - 1)], 0) == 1

    @pl.when(plane == 0)
    def _():
        optical[...] = above[...]
        for ref in (mh, ml, nh, nl):
            edge = jnp.zeros((ref.shape[0], 128), BF)
            ref[:, :128] = edge
            ref[:, ref.shape[1] - 128 :] = edge

    for joined, far, packed, at in (
        (join_top, above_top, rim_top, 0),
        (join_bot, above_bot, rim_bot, rows + rim),
    ):
        value = jnp.where(joined, jnp.exp(-far[...]) * packed[0, :rim], 0.0)
        wh[at : at + rim], wl[at : at + rim] = split(value)
    for r in range(0, rows, 64):
        depth = optical[r : r + 64]
        value = jnp.exp(-depth) * est[0, r : r + 64]
        wh[rim + r : rim + r + 64], wl[rim + r : rim + r + 64] = split(value)
        optical[r : r + 64] = depth + ext[0, r : r + 64]

    def vertical(way, sh, sl, dh, dl):
        total = dh.shape[0]
        for at in range(0, total, 192):
            m = min(192, total - at)
            depth = min(256, m + rim)
            th, tl = v_ref[0, way, 0, :m, :depth], v_ref[0, way, 1, :m, :depth]
            for c in range(0, cols, 256):
                result = dot3(th, tl, sh[at : at + depth, c : c + 256], sl[at : at + depth, c : c + 256])
                dh[at : at + m, 128 + c : 384 + c], dl[at : at + m, 128 + c : 384 + c] = split(result)

    vertical(0, wh, wl, mh, ml)
    lh, ll = l_ref.at[0, 0, 0], l_ref.at[0, 0, 1]
    for c in range(0, cols, 256):
        for a, b in ((0, 160), (160, 320)):
            blurred = dot3(mh[a:b, c : c + 512], ml[a:b, c : c + 512], lh[...], ll[...])
            s = slice(c, c + 256)
            if a == 0:
                halo = jnp.where(join_top, rim_top[0, rim:, s] / blurred[:HALF], 0.0)
                inner = mea[0, : b - HALF, s] / blurred[HALF:]
                qh[:HALF, s], ql[:HALF, s] = split(halo)
                qh[HALF:b, s], ql[HALF:b, s] = split(inner)
            else:
                halo = jnp.where(join_bot, rim_bot[0, rim:, s] / blurred[b - a - HALF :], 0.0)
                inner = mea[0, a - HALF :, s] / blurred[: b - a - HALF]
                qh[b - HALF :, s], ql[b - HALF :, s] = split(halo)
                qh[a : b - HALF, s], ql[a : b - HALF, s] = split(inner)

    vertical(1, qh, ql, nh, nl)
    lh, ll = l_ref.at[0, 1, 0], l_ref.at[0, 1, 1]
    for c in range(0, cols, 256):
        s = slice(c, c + 256)
        for a in range(0, rows, 128):
            t = slice(a, a + 128)
            spread = dot3(nh[t, c : c + 512], nl[t, c : c + 512], lh[...], ll[...])
            result = est[0, t, s] * spread
            upd[0, t, s] = result
            top[t, s] = jnp.maximum(jnp.where(plane == 0, result, top[t, s]), result)

    @pl.when(plane == pl.num_programs(0) - 1)
    def _():
        quarter = rows // 4
        for piece, (keep, give) in enumerate(((o0, o1), (o2, o3))):
            kept = side(piece)
            keep[...] = top[rows_at(2 * piece + kept, quarter)]
            give[...] = top[rows_at(2 * piece + 1 - kept, quarter)]


def step(seams, ext, est, mea, above, above_top, above_bot, rim_top, rim_bot, v, l):
    planes, rows, cols = ext.shape
    rim, quarter = 2 * HALF, rows // 4
    stack = pl.BlockSpec((1, rows, cols), lambda p: (p, 0, 0))
    pack = pl.BlockSpec((1, rim + HALF, cols), lambda p: (p, 0, 0))
    part = pl.BlockSpec((quarter, cols), lambda p: (0, 0))
    return pl.pallas_call(
        step_kernel,
        grid=(planes,),
        in_specs=[
            smem(), stack, stack, stack, whole(), whole(), whole(), pack, pack,
            pl.BlockSpec((1,) + v.shape[1:], lambda p: (p, 0, 0, 0, 0)),
            pl.BlockSpec((1,) + l.shape[1:], lambda p: (p, 0, 0, 0, 0)),
        ],
        out_specs=[stack] + [part] * 4,
        out_shape=[jax.ShapeDtypeStruct((planes, rows, cols), F32)]
        + [jax.ShapeDtypeStruct((quarter, cols), F32)] * 4,
        scratch_shapes=[
            pltpu.VMEM((rows, cols), F32),
            pltpu.VMEM((rows, cols), F32),
            pltpu.VMEM((rows + 2 * rim, cols), BF),
            pltpu.VMEM((rows + 2 * rim, cols), BF),
            pltpu.VMEM((rows + rim, cols + 256), BF),
            pltpu.VMEM((rows + rim, cols + 256), BF),
            pltpu.VMEM((rows + rim, cols), BF),
            pltpu.VMEM((rows + rim, cols), BF),
            pltpu.VMEM((rows, cols + 256), BF),
            pltpu.VMEM((rows, cols + 256), BF),
        ],
        compiler_params=params(44),
        cost_estimate=pl.CostEstimate(flops=12 << 30, bytes_accessed=24 << 20, transcendentals=1 << 20),
    )(seams, ext, est, mea, above, above_top, above_bot, rim_top, rim_bot, v, l)


def on_device(measured, estimate, extinction, psf_rows, psf_cols, stratum, seam_flags):
    rows = measured.shape[1]
    rim = 2 * HALF
    tiles = lax.axis_size("tile")
    onward = [(i, i + 1) for i in range(tiles - 1)]
    backward = [(i + 1, i) for i in range(tiles - 1)]
    above, (v, l) = above_of(sums(extinction), bands(psf_rows, psf_cols, stratum))
    up, down = rims(extinction, estimate, measured)
    rim_top = lax.ppermute(down, "tile", onward)
    rim_bot = lax.ppermute(up, "tile", backward)
    above_top = lax.ppermute(above[rows - rim :], "tile", onward)
    above_bot = lax.ppermute(above[:rim], "tile", backward)
    updated, keep_a, give_a, keep_b, give_b = step(
        seam_flags, extinction, estimate, measured, above, above_top, above_bot, rim_top, rim_bot, v, l
    )
    return updated, highest([(keep_a, give_a), (keep_b, give_b)])


def solution(mesh):
    return jax.shard_map(
        on_device,
        mesh=mesh,
        in_specs=(
            P("depth", "tile", None),
            P("depth", "tile", None),
            P("depth", "tile", None),
            P(),
            P(),
            P("depth"),
            P(),
        ),
        out_specs=(P("depth", "tile", None), P("tile", None)),
        check_vma=False,
    )
```

```python
import jax
import jax.numpy as jnp
from jax import lax
from jax.experimental import pallas as pl
from jax.experimental.pallas import tpu as pltpu
from jax.sharding import PartitionSpec as P

SIDE = 4
HALF = 32
TAPS = 65
BF = jnp.bfloat16
F32 = jnp.float32


def params(mib):
    return pltpu.CompilerParams(vmem_limit_bytes=mib << 20)


def whole():
    return pl.BlockSpec(memory_space=pltpu.VMEM)


def smem():
    return pl.BlockSpec(memory_space=pltpu.SMEM)


PAIRINGS = (
    (("y", 1), ("y", 3), ("x", 1), ("x", 3)),
    (("x", 1), ("x", 3), ("y", 1), ("y", 3)),
)


def pairs(piece, number, tiles):
    result = []
    for x in range(SIDE):
        for y in range(SIDE):
            for tile in range(tiles):
                axis, flip = PAIRINGS[piece][number]
                tx, ty = (x, y ^ flip) if axis == "y" else (x ^ flip, y)
                result.append(((x * SIDE + y) * tiles + tile, (tx * SIDE + ty) * tiles + tile))
    return result


def swap(value, piece, number):
    return lax.ppermute(value, ("depth", "tile"), pairs(piece, number, lax.axis_size("tile")))


def side(piece):
    depth = lax.axis_index("depth")
    axis, _ = PAIRINGS[piece][0]
    value = depth % SIDE if axis == "y" else depth // SIDE
    return (value + 1) // 2 % 2


def split(value):
    high = value.astype(BF)
    return high, (value - high.astype(F32)).astype(BF)


def rows_at(index, size):
    return pl.ds(pl.multiple_of(index * size, size), size)


def sums_kernel(ext, out, buf, sems):
    block = out.shape[0] // sems.shape[0]
    copies = []
    for i in range(sems.shape[0]):
        rows = pl.ds(i * block, block)
        copies.append(pltpu.make_async_copy(ext.at[:, rows], buf.at[:, rows], sems.at[i]))
        copies[-1].start()
    for i, copy in enumerate(copies):
        copy.wait()
        rows = pl.ds(i * block, block)
        total = buf[0, rows]
        for plane in range(1, buf.shape[0]):
            total = total + buf[plane, rows]
        out[rows] = total


def sums(extinction):
    planes, rows, cols = extinction.shape
    return pl.pallas_call(
        sums_kernel,
        in_specs=[pl.BlockSpec(memory_space=pl.ANY)],
        out_specs=whole(),
        out_shape=jax.ShapeDtypeStruct((rows, cols), F32),
        scratch_shapes=[pltpu.VMEM((planes, rows, cols), F32), pltpu.SemaphoreType.DMA((8,))],
        compiler_params=params(60),
    )(extinction)


def rims_kernel(ext, est, mea, up, down, ext_buf, est_buf, mea_buf, sems):
    rim = 2 * HALF
    planes, rows, _ = ext.shape
    ends = ((0, 0, up), (rows - rim, rows - HALF, down))
    copies = []
    for i, (wide, narrow, _) in enumerate(ends):
        for j, (source, buf, at, size) in enumerate(
            ((ext, ext_buf, wide, rim), (est, est_buf, wide, rim), (mea, mea_buf, narrow, HALF))
        ):
            copies.append(pltpu.make_async_copy(source.at[:, pl.ds(at, size)], buf.at[i], sems.at[3 * i + j]))
            copies[-1].start()
    for i, (_, _, out) in enumerate(ends):
        for copy in copies[3 * i : 3 * i + 3]:
            copy.wait()
        depth = jnp.zeros(ext_buf.shape[2:], F32)
        for plane in range(planes):
            out[plane, :rim] = jnp.exp(-depth) * est_buf[i, plane]
            out[plane, rim:] = mea_buf[i, plane]
            depth = depth + ext_buf[i, plane]


def rims(extinction, estimate, measured):
    planes, rows, cols = extinction.shape
    rim = 2 * HALF
    return pl.pallas_call(
        rims_kernel,
        in_specs=[pl.BlockSpec(memory_space=pl.ANY)] * 3,
        out_specs=[whole()] * 2,
        out_shape=[jax.ShapeDtypeStruct((planes, rim + HALF, cols), F32)] * 2,
        scratch_shapes=[
            pltpu.VMEM((2, planes, rim, cols), F32),
            pltpu.VMEM((2, planes, rim, cols), F32),
            pltpu.VMEM((2, planes, HALF, cols), F32),
            pltpu.SemaphoreType.DMA((6,)),
        ],
        compiler_params=params(60),
        cost_estimate=pl.CostEstimate(flops=1 << 20, bytes_accessed=8 << 20, transcendentals=1 << 19),
    )(extinction, estimate, measured)


def scan_kernel(parts, out):
    running = jnp.zeros(parts.shape[1:], F32)
    for slab in range(parts.shape[0]):
        value = parts[slab]
        out[slab] = running
        running = running + value


def above_of(total, meanwhile):
    rows, cols = total.shape
    slabs = lax.axis_size("depth")
    parts = total.reshape(slabs, rows // slabs, cols)
    parts = lax.all_to_all(parts, "depth", 0, 0, tiled=True)
    prefixes = pl.pallas_call(
        scan_kernel,
        in_specs=[whole()],
        out_specs=whole(),
        out_shape=jax.ShapeDtypeStruct(parts.shape, F32),
        compiler_params=params(16),
    )(parts)
    prefixes, meanwhile = lax.optimization_barrier((prefixes, meanwhile))
    return lax.all_to_all(prefixes, "depth", 0, 0, tiled=True).reshape(rows, cols), meanwhile


def highest(parts):
    joined = []
    held = [jnp.maximum(keep, swap(give, piece, 0)) for piece, (keep, give) in enumerate(parts)]
    for number in range(1, 4):
        held = [jnp.maximum(value, swap(value, piece, number)) for piece, value in enumerate(held)]
    for piece, mine in enumerate(held):
        other = swap(mine, piece, 0)
        first = side(piece) == 0
        joined += [jnp.where(first, mine, other), jnp.where(first, other, mine)]
    return jnp.concatenate(joined)


def bands_kernel(stratum, taps, v_ref, l_ref):
    def toeplitz(row, count, shift):
        line = taps[0, row : row + 1]
        line = line / jnp.sum(line, axis=1, keepdims=True)
        wide = jnp.broadcast_to(line, (count, line.shape[1]))
        return pltpu.roll(wide, shift, 1, stride=1, stride_axis=0)

    for way in range(2):
        band = toeplitz(way, v_ref.shape[3], 0)
        v_ref[0, way, 0], v_ref[0, way, 1] = split(band)
        ring = toeplitz(3 - way, 256, 256 - HALF)
        k = lax.broadcasted_iota(jnp.int32, ring.shape, 0)
        n = lax.broadcasted_iota(jnp.int32, ring.shape, 1)
        zero = jnp.zeros_like(ring)
        main = jnp.where(jnp.abs(n - k) <= HALF, ring, zero)
        left = jnp.where(k - n > HALF, ring, zero)[128:]
        right = jnp.where(n - k > HALF, ring, zero)[:128]
        l_ref[0, way, :256], l_ref[0, way, 256:512] = split(main)
        high, low = split(left + right)
        pair = jnp.concatenate([high[:HALF], high[128 - HALF :]], axis=0)
        l_ref[0, way, 512 : 512 + 2 * HALF] = pair
        l_ref[0, way, 512 + 2 * HALF : 640] = pair
        l_ref[0, way, 640:] = low


def bands(psf_rows, psf_cols, stratum):
    planes = stratum.shape[0]
    taps = jnp.stack([psf_rows, psf_rows[:, ::-1], psf_cols, psf_cols[:, ::-1]], axis=1)
    taps = jnp.pad(taps, ((0, 0), (0, 0), (0, 256 - TAPS)))
    return pl.pallas_call(
        bands_kernel,
        grid_spec=pltpu.PrefetchScalarGridSpec(
            num_scalar_prefetch=1,
            grid=(planes,),
            in_specs=[pl.BlockSpec((1, 4, 256), lambda p, s: (s[p], 0, 0))],
            out_specs=[
                pl.BlockSpec((1, 2, 2, 192, 256), lambda p, s: (p, 0, 0, 0, 0)),
                pl.BlockSpec((1, 2, 768, 256), lambda p, s: (p, 0, 0, 0)),
            ],
        ),
        out_shape=[
            jax.ShapeDtypeStruct((planes, 2, 2, 192, 256), BF),
            jax.ShapeDtypeStruct((planes, 2, 768, 256), BF),
        ],
        compiler_params=params(60),
        cost_estimate=pl.CostEstimate(flops=1 << 22, bytes_accessed=6 << 20, transcendentals=0),
    )(stratum, taps)


def dot(a, b):
    return jnp.dot(a, b, preferred_element_type=F32)


def corners(high, low, out):
    for c in range(0, out.shape[1], 256):
        left, right = slice(c, c + 128), slice(c + 384, c + 512)
        for r in range(0, out.shape[0], 64):
            t = slice(r, r + 64)
            lane = lax.broadcasted_iota(jnp.int32, (64, 128), 1)
            near = lane < 64
            h = jnp.where(near, high[t, right].astype(F32), high[t, left].astype(F32))
            w = jnp.where(near, low[t, right].astype(F32), low[t, left].astype(F32))
            between = (lane >= HALF) & (lane < 128 - HALF)
            out[t, c : c + 128] = jnp.where(between, pltpu.roll(w, 64, 1), h).astype(BF)
            out[t, c + 128 : c + 256] = h.astype(BF)


def lateral(high, low, corner, rows, c, band):
    s = slice(c + 128, c + 384)
    source = jnp.concatenate(
        [high[rows, s], high[rows, s], low[rows, s], corner[rows, c : c + 256]], axis=1
    )
    weights = jnp.concatenate([band[:512], band[:256], band[512:]], axis=0)
    return dot(source, weights)


def step_kernel(
    seams, ext, est, mea, above, above_top, above_bot, rim_top, rim_bot, v_ref, l_ref,
    upd, o0, o1, o2, o3, optical, top, wh, wl, mh, ml, qh, ql, nh, nl, corner,
):
    plane = pl.program_id(0)
    tile = lax.axis_index("tile")
    rows, cols = optical.shape
    rim = 2 * HALF
    ends = lax.axis_size("tile") - 1
    join_top = jnp.where(tile > 0, seams[jnp.maximum(tile - 1, 0)], 0) == 1
    join_bot = jnp.where(tile < ends, seams[jnp.minimum(tile, ends - 1)], 0) == 1

    @pl.when(plane == 0)
    def _():
        optical[...] = above[...]
        for ref in (mh, ml, nh, nl):
            edge = jnp.zeros((ref.shape[0], 128), BF)
            ref[:, :128] = edge
            ref[:, ref.shape[1] - 128 :] = edge

    for joined, far, packed, at in (
        (join_top, above_top, rim_top, 0),
        (join_bot, above_bot, rim_bot, rows + rim),
    ):
        value = jnp.where(joined, jnp.exp(-far[...]) * packed[0, :rim], 0.0)
        wh[at : at + rim], wl[at : at + rim] = split(value)
    for r in range(0, rows, 64):
        depth = optical[r : r + 64]
        value = jnp.exp(-depth) * est[0, r : r + 64]
        wh[rim + r : rim + r + 64], wl[rim + r : rim + r + 64] = split(value)
        optical[r : r + 64] = depth + ext[0, r : r + 64]

    def vertical(way, sh, sl, dh, dl):
        total = dh.shape[0]
        for at in range(0, total, 192):
            m = min(192, total - at)
            depth = min(256, m + rim)
            th, tl = v_ref[0, way, 0, :m, :depth], v_ref[0, way, 1, :m, :depth]
            for c in range(0, cols, 256):
                both = dot(jnp.concatenate([th, tl], axis=0), sh[at : at + depth, c : c + 256])
                result = both[:m] + (both[m:] + dot(th, sl[at : at + depth, c : c + 256]))
                dh[at : at + m, 128 + c : 384 + c], dl[at : at + m, 128 + c : 384 + c] = split(result)

    vertical(0, wh, wl, mh, ml)
    corners(mh, ml, corner)
    for c in range(0, cols, 256):
        s = slice(c, c + 256)
        blurred = lateral(mh, ml, corner, slice(0, rows + rim), c, l_ref.at[0, 0])
        q0 = jnp.where(join_top, rim_top[0, rim:, s] / blurred[:HALF], 0.0)
        q1 = mea[0, :, s] / blurred[HALF : HALF + rows]
        q2 = jnp.where(join_bot, rim_bot[0, rim:, s] / blurred[HALF + rows :], 0.0)
        qh[:HALF, s], ql[:HALF, s] = split(q0)
        qh[HALF : HALF + rows, s], ql[HALF : HALF + rows, s] = split(q1)
        qh[HALF + rows :, s], ql[HALF + rows :, s] = split(q2)

    vertical(1, qh, ql, nh, nl)
    ours = corner.at[pl.ds(0, rows)]
    corners(nh, nl, ours)
    for c in range(0, cols, 256):
        s = slice(c, c + 256)
        result = est[0, :, s] * lateral(nh, nl, ours, slice(0, rows), c, l_ref.at[0, 1])
        upd[0, :, s] = result
        top[:, s] = jnp.maximum(jnp.where(plane == 0, result, top[:, s]), result)

    @pl.when(plane == pl.num_programs(0) - 1)
    def _():
        quarter = rows // 4
        for piece, (keep, give) in enumerate(((o0, o1), (o2, o3))):
            kept = side(piece)
            keep[...] = top[rows_at(2 * piece + kept, quarter)]
            give[...] = top[rows_at(2 * piece + 1 - kept, quarter)]


def step(seams, ext, est, mea, above, above_top, above_bot, rim_top, rim_bot, v, l):
    planes, rows, cols = ext.shape
    rim, quarter = 2 * HALF, rows // 4
    stack = pl.BlockSpec((1, rows, cols), lambda p: (p, 0, 0))
    pack = pl.BlockSpec((1, rim + HALF, cols), lambda p: (p, 0, 0))
    part = pl.BlockSpec((quarter, cols), lambda p: (0, 0))
    return pl.pallas_call(
        step_kernel,
        grid=(planes,),
        in_specs=[
            smem(), stack, stack, stack, whole(), whole(), whole(), pack, pack,
            pl.BlockSpec((1,) + v.shape[1:], lambda p: (p, 0, 0, 0, 0)),
            pl.BlockSpec((1,) + l.shape[1:], lambda p: (p, 0, 0, 0)),
        ],
        out_specs=[stack] + [part] * 4,
        out_shape=[jax.ShapeDtypeStruct((planes, rows, cols), F32)]
        + [jax.ShapeDtypeStruct((quarter, cols), F32)] * 4,
        scratch_shapes=[
            pltpu.VMEM((rows, cols), F32),
            pltpu.VMEM((rows, cols), F32),
            pltpu.VMEM((rows + 2 * rim, cols), BF),
            pltpu.VMEM((rows + 2 * rim, cols), BF),
            pltpu.VMEM((rows + rim, cols + 256), BF),
            pltpu.VMEM((rows + rim, cols + 256), BF),
            pltpu.VMEM((rows + rim, cols), BF),
            pltpu.VMEM((rows + rim, cols), BF),
            pltpu.VMEM((rows, cols + 256), BF),
            pltpu.VMEM((rows, cols + 256), BF),
            pltpu.VMEM((rows + rim, cols), BF),
        ],
        compiler_params=params(44),
        cost_estimate=pl.CostEstimate(flops=12 << 30, bytes_accessed=24 << 20, transcendentals=1 << 20),
    )(seams, ext, est, mea, above, above_top, above_bot, rim_top, rim_bot, v, l)


def on_device(measured, estimate, extinction, psf_rows, psf_cols, stratum, seam_flags):
    rows = measured.shape[1]
    rim = 2 * HALF
    tiles = lax.axis_size("tile")
    onward = [(i, i + 1) for i in range(tiles - 1)]
    backward = [(i + 1, i) for i in range(tiles - 1)]
    above, (v, l) = above_of(sums(extinction), bands(psf_rows, psf_cols, stratum))
    up, down = rims(extinction, estimate, measured)
    rim_top = lax.ppermute(down, "tile", onward)
    rim_bot = lax.ppermute(up, "tile", backward)
    above_top = lax.ppermute(above[rows - rim :], "tile", onward)
    above_bot = lax.ppermute(above[:rim], "tile", backward)
    updated, keep_a, give_a, keep_b, give_b = step(
        seam_flags, extinction, estimate, measured, above, above_top, above_bot, rim_top, rim_bot, v, l
    )
    return updated, highest([(keep_a, give_a), (keep_b, give_b)])


def solution(mesh):
    return jax.shard_map(
        on_device,
        mesh=mesh,
        in_specs=(
            P("depth", "tile", None),
            P("depth", "tile", None),
            P("depth", "tile", None),
            P(),
            P(),
            P("depth"),
            P(),
        ),
        out_specs=(P("depth", "tile", None), P("tile", None)),
        check_vma=False,
    )
```

```python
import jax
import jax.numpy as jnp
from jax import lax
from jax.experimental import pallas as pl
from jax.experimental.pallas import tpu as pltpu
from jax.sharding import PartitionSpec as P

SIDE = 4
HALF = 32
TAPS = 65
BF = jnp.bfloat16
F32 = jnp.float32


def params(mib):
    return pltpu.CompilerParams(vmem_limit_bytes=mib << 20)


def whole():
    return pl.BlockSpec(memory_space=pltpu.VMEM)


def smem():
    return pl.BlockSpec(memory_space=pltpu.SMEM)


PAIRINGS = (
    (("y", 1), ("y", 3), ("x", 1), ("x", 3)),
    (("x", 1), ("x", 3), ("y", 1), ("y", 3)),
)


def pairs(piece, number, tiles):
    result = []
    for x in range(SIDE):
        for y in range(SIDE):
            for tile in range(tiles):
                axis, flip = PAIRINGS[piece][number]
                tx, ty = (x, y ^ flip) if axis == "y" else (x ^ flip, y)
                result.append(((x * SIDE + y) * tiles + tile, (tx * SIDE + ty) * tiles + tile))
    return result


def swap(value, piece, number):
    return lax.ppermute(value, ("depth", "tile"), pairs(piece, number, lax.axis_size("tile")))


def side(piece):
    depth = lax.axis_index("depth")
    axis, _ = PAIRINGS[piece][0]
    value = depth % SIDE if axis == "y" else depth // SIDE
    return (value + 1) // 2 % 2


def split(value):
    high = value.astype(BF)
    return high, (value - high.astype(F32)).astype(BF)


def rows_at(index, size):
    return pl.ds(pl.multiple_of(index * size, size), size)


def sums_kernel(ext, out, buf, sems):
    block = out.shape[0] // sems.shape[0]
    copies = []
    for i in range(sems.shape[0]):
        rows = pl.ds(i * block, block)
        copies.append(pltpu.make_async_copy(ext.at[:, rows], buf.at[:, rows], sems.at[i]))
        copies[-1].start()
    for i, copy in enumerate(copies):
        copy.wait()
        rows = pl.ds(i * block, block)
        total = buf[0, rows]
        for plane in range(1, buf.shape[0]):
            total = total + buf[plane, rows]
        out[rows] = total


def sums(extinction):
    planes, rows, cols = extinction.shape
    return pl.pallas_call(
        sums_kernel,
        in_specs=[pl.BlockSpec(memory_space=pl.ANY)],
        out_specs=whole(),
        out_shape=jax.ShapeDtypeStruct((rows, cols), F32),
        scratch_shapes=[pltpu.VMEM((planes, rows, cols), F32), pltpu.SemaphoreType.DMA((8,))],
        compiler_params=params(60),
    )(extinction)


def rims_kernel(ext, est, mea, beside, across, ext_buf, est_buf, mea_buf, sems):
    rim = 2 * HALF
    planes, rows, _ = ext.shape
    core = lax.axis_index("tile") % 2
    ends = []
    for at_far, out in ((core == 0, beside), (core == 1, across)):
        wide = pl.multiple_of(jnp.where(at_far, rows - rim, 0), HALF)
        narrow = pl.multiple_of(jnp.where(at_far, rows - HALF, 0), HALF)
        ends.append((wide, narrow, out))
    copies = []
    for i, (wide, narrow, _) in enumerate(ends):
        for j, (source, buf, at, size) in enumerate(
            ((ext, ext_buf, wide, rim), (est, est_buf, wide, rim), (mea, mea_buf, narrow, HALF))
        ):
            copies.append(pltpu.make_async_copy(source.at[:, pl.ds(at, size)], buf.at[i], sems.at[3 * i + j]))
            copies[-1].start()
    for i, (_, _, out) in enumerate(ends):
        for copy in copies[3 * i : 3 * i + 3]:
            copy.wait()
        depth = jnp.zeros(ext_buf.shape[2:], F32)
        for plane in range(planes):
            out[plane, :rim] = jnp.exp(-depth) * est_buf[i, plane]
            out[plane, rim:] = mea_buf[i, plane]
            depth = depth + ext_buf[i, plane]


def rims(extinction, estimate, measured):
    planes, rows, cols = extinction.shape
    rim = 2 * HALF
    return pl.pallas_call(
        rims_kernel,
        in_specs=[pl.BlockSpec(memory_space=pl.ANY)] * 3,
        out_specs=[whole()] * 2,
        out_shape=[jax.ShapeDtypeStruct((planes, rim + HALF, cols), F32)] * 2,
        scratch_shapes=[
            pltpu.VMEM((2, planes, rim, cols), F32),
            pltpu.VMEM((2, planes, rim, cols), F32),
            pltpu.VMEM((2, planes, HALF, cols), F32),
            pltpu.SemaphoreType.DMA((6,)),
        ],
        compiler_params=params(60),
        cost_estimate=pl.CostEstimate(flops=1 << 20, bytes_accessed=8 << 20, transcendentals=1 << 19),
    )(extinction, estimate, measured)


def scan_kernel(parts, out):
    running = jnp.zeros(parts.shape[1:], F32)
    for slab in range(parts.shape[0]):
        value = parts[slab]
        out[slab] = running
        running = running + value


def above_of(total, meanwhile):
    rows, cols = total.shape
    slabs = lax.axis_size("depth")
    parts = total.reshape(slabs, rows // slabs, cols)
    parts = lax.all_to_all(parts, "depth", 0, 0, tiled=True)
    prefixes = pl.pallas_call(
        scan_kernel,
        in_specs=[whole()],
        out_specs=whole(),
        out_shape=jax.ShapeDtypeStruct(parts.shape, F32),
        compiler_params=params(16),
    )(parts)
    prefixes, meanwhile = lax.optimization_barrier((prefixes, meanwhile))
    return lax.all_to_all(prefixes, "depth", 0, 0, tiled=True).reshape(rows, cols), meanwhile


def highest(parts):
    joined = []
    held = [jnp.maximum(keep, swap(give, piece, 0)) for piece, (keep, give) in enumerate(parts)]
    for number in range(1, 4):
        held = [jnp.maximum(value, swap(value, piece, number)) for piece, value in enumerate(held)]
    for piece, mine in enumerate(held):
        other = swap(mine, piece, 0)
        first = side(piece) == 0
        joined += [jnp.where(first, mine, other), jnp.where(first, other, mine)]
    return jnp.concatenate(joined)


def bands_kernel(stratum, taps, v_ref, l_ref):
    def toeplitz(row, count, shift):
        line = taps[0, row : row + 1]
        line = line / jnp.sum(line, axis=1, keepdims=True)
        wide = jnp.broadcast_to(line, (count, line.shape[1]))
        return pltpu.roll(wide, shift, 1, stride=1, stride_axis=0)

    for way in range(2):
        band = toeplitz(way, v_ref.shape[3], 0)
        v_ref[0, way, 0], v_ref[0, way, 1] = split(band)
        ring = toeplitz(3 - way, 256, 256 - HALF)
        k = lax.broadcasted_iota(jnp.int32, ring.shape, 0)
        n = lax.broadcasted_iota(jnp.int32, ring.shape, 1)
        zero = jnp.zeros_like(ring)
        main = jnp.where(jnp.abs(n - k) <= HALF, ring, zero)
        left = jnp.where(k - n > HALF, ring, zero)[128:]
        right = jnp.where(n - k > HALF, ring, zero)[:128]
        l_ref[0, way, :256], l_ref[0, way, 256:512] = split(main)
        high, low = split(left + right)
        pair = jnp.concatenate([high[:HALF], high[128 - HALF :]], axis=0)
        l_ref[0, way, 512 : 512 + 2 * HALF] = pair
        l_ref[0, way, 512 + 2 * HALF : 640] = pair
        l_ref[0, way, 640:] = low


def bands(psf_rows, psf_cols, stratum):
    planes = stratum.shape[0]
    taps = jnp.stack([psf_rows, psf_rows[:, ::-1], psf_cols, psf_cols[:, ::-1]], axis=1)
    taps = jnp.pad(taps, ((0, 0), (0, 0), (0, 256 - TAPS)))
    return pl.pallas_call(
        bands_kernel,
        grid_spec=pltpu.PrefetchScalarGridSpec(
            num_scalar_prefetch=1,
            grid=(planes,),
            in_specs=[pl.BlockSpec((1, 4, 256), lambda p, s: (s[p], 0, 0))],
            out_specs=[
                pl.BlockSpec((1, 2, 2, 192, 256), lambda p, s: (p, 0, 0, 0, 0)),
                pl.BlockSpec((1, 2, 768, 256), lambda p, s: (p, 0, 0, 0)),
            ],
        ),
        out_shape=[
            jax.ShapeDtypeStruct((planes, 2, 2, 192, 256), BF),
            jax.ShapeDtypeStruct((planes, 2, 768, 256), BF),
        ],
        compiler_params=params(60),
        cost_estimate=pl.CostEstimate(flops=1 << 22, bytes_accessed=6 << 20, transcendentals=0),
    )(stratum, taps)


def dot(a, b):
    return jnp.dot(a, b, preferred_element_type=F32)


def corners(high, low, out):
    for c in range(0, out.shape[1], 256):
        left, right = slice(c, c + 128), slice(c + 384, c + 512)
        for r in range(0, out.shape[0], 64):
            t = slice(r, r + 64)
            lane = lax.broadcasted_iota(jnp.int32, (64, 128), 1)
            near = lane < 64
            h = jnp.where(near, high[t, right].astype(F32), high[t, left].astype(F32))
            w = jnp.where(near, low[t, right].astype(F32), low[t, left].astype(F32))
            between = (lane >= HALF) & (lane < 128 - HALF)
            out[t, c : c + 128] = jnp.where(between, pltpu.roll(w, 64, 1), h).astype(BF)
            out[t, c + 128 : c + 256] = h.astype(BF)


def lateral(high, low, corner, rows, c, band):
    s = slice(c + 128, c + 384)
    source = jnp.concatenate(
        [high[rows, s], high[rows, s], low[rows, s], corner[rows, c : c + 256]], axis=1
    )
    weights = jnp.concatenate([band[:512], band[:256], band[512:]], axis=0)
    return dot(source, weights)


def step_kernel(
    seams, ext, est, mea, above, above_across, above_beside, rim_across, rim_beside, v_ref, l_ref,
    upd, o0, o1, o2, o3, optical, top, wh, wl, mh, ml, qh, ql, nh, nl, corner,
):
    plane = pl.program_id(0)
    tile = lax.axis_index("tile")
    rows, cols = optical.shape
    rim = 2 * HALF
    ends = lax.axis_size("tile") - 1
    join_top = jnp.where(tile > 0, seams[jnp.maximum(tile - 1, 0)], 0) == 1
    join_bot = jnp.where(tile < ends, seams[jnp.minimum(tile, ends - 1)], 0) == 1

    @pl.when(plane == 0)
    def _():
        optical[...] = above[...]
        for ref in (mh, ml, nh, nl):
            edge = jnp.zeros((ref.shape[0], 128), BF)
            ref[:, :128] = edge
            ref[:, ref.shape[1] - 128 :] = edge

    core = tile % 2

    def top_of(across, beside):
        return jnp.where(core == 0, across, beside)

    def bot_of(across, beside):
        return jnp.where(core == 0, beside, across)

    for joined, pick, at in ((join_top, top_of, 0), (join_bot, bot_of, rows + rim)):
        far = pick(above_across[...], above_beside[...])
        packed = pick(rim_across[0, :rim], rim_beside[0, :rim])
        value = jnp.where(joined, jnp.exp(-far) * packed, 0.0)
        wh[at : at + rim], wl[at : at + rim] = split(value)
    for r in range(0, rows, 64):
        depth = optical[r : r + 64]
        value = jnp.exp(-depth) * est[0, r : r + 64]
        wh[rim + r : rim + r + 64], wl[rim + r : rim + r + 64] = split(value)
        optical[r : r + 64] = depth + ext[0, r : r + 64]

    def vertical(way, sh, sl, dh, dl):
        total = dh.shape[0]
        for at in range(0, total, 192):
            m = min(192, total - at)
            depth = min(256, m + rim)
            th, tl = v_ref[0, way, 0, :m, :depth], v_ref[0, way, 1, :m, :depth]
            for c in range(0, cols, 256):
                both = dot(jnp.concatenate([th, tl], axis=0), sh[at : at + depth, c : c + 256])
                result = both[:m] + (both[m:] + dot(th, sl[at : at + depth, c : c + 256]))
                dh[at : at + m, 128 + c : 384 + c], dl[at : at + m, 128 + c : 384 + c] = split(result)

    vertical(0, wh, wl, mh, ml)
    corners(mh, ml, corner)
    for c in range(0, cols, 256):
        s = slice(c, c + 256)
        blurred = lateral(mh, ml, corner, slice(0, rows + rim), c, l_ref.at[0, 0])
        q0 = top_of(rim_across[0, rim:, s], rim_beside[0, rim:, s]) / blurred[:HALF]
        q0 = jnp.where(join_top, q0, 0.0)
        q1 = mea[0, :, s] / blurred[HALF : HALF + rows]
        q2 = bot_of(rim_across[0, rim:, s], rim_beside[0, rim:, s]) / blurred[HALF + rows :]
        q2 = jnp.where(join_bot, q2, 0.0)
        qh[:HALF, s], ql[:HALF, s] = split(q0)
        qh[HALF : HALF + rows, s], ql[HALF : HALF + rows, s] = split(q1)
        qh[HALF + rows :, s], ql[HALF + rows :, s] = split(q2)

    vertical(1, qh, ql, nh, nl)
    ours = corner.at[pl.ds(0, rows)]
    corners(nh, nl, ours)
    for c in range(0, cols, 256):
        s = slice(c, c + 256)
        result = est[0, :, s] * lateral(nh, nl, ours, slice(0, rows), c, l_ref.at[0, 1])
        upd[0, :, s] = result
        top[:, s] = jnp.maximum(jnp.where(plane == 0, result, top[:, s]), result)

    @pl.when(plane == pl.num_programs(0) - 1)
    def _():
        quarter = rows // 4
        for piece, (keep, give) in enumerate(((o0, o1), (o2, o3))):
            kept = side(piece)
            keep[...] = top[rows_at(2 * piece + kept, quarter)]
            give[...] = top[rows_at(2 * piece + 1 - kept, quarter)]


def step(seams, ext, est, mea, above, above_across, above_beside, rim_across, rim_beside, v, l):
    planes, rows, cols = ext.shape
    rim, quarter = 2 * HALF, rows // 4
    stack = pl.BlockSpec((1, rows, cols), lambda p: (p, 0, 0))
    pack = pl.BlockSpec((1, rim + HALF, cols), lambda p: (p, 0, 0))
    part = pl.BlockSpec((quarter, cols), lambda p: (0, 0))
    return pl.pallas_call(
        step_kernel,
        grid=(planes,),
        in_specs=[
            smem(), stack, stack, stack, whole(), whole(), whole(), pack, pack,
            pl.BlockSpec((1,) + v.shape[1:], lambda p: (p, 0, 0, 0, 0)),
            pl.BlockSpec((1,) + l.shape[1:], lambda p: (p, 0, 0, 0)),
        ],
        out_specs=[stack] + [part] * 4,
        out_shape=[jax.ShapeDtypeStruct((planes, rows, cols), F32)]
        + [jax.ShapeDtypeStruct((quarter, cols), F32)] * 4,
        scratch_shapes=[
            pltpu.VMEM((rows, cols), F32),
            pltpu.VMEM((rows, cols), F32),
            pltpu.VMEM((rows + 2 * rim, cols), BF),
            pltpu.VMEM((rows + 2 * rim, cols), BF),
            pltpu.VMEM((rows + rim, cols + 256), BF),
            pltpu.VMEM((rows + rim, cols + 256), BF),
            pltpu.VMEM((rows + rim, cols), BF),
            pltpu.VMEM((rows + rim, cols), BF),
            pltpu.VMEM((rows, cols + 256), BF),
            pltpu.VMEM((rows, cols + 256), BF),
            pltpu.VMEM((rows + rim, cols), BF),
        ],
        compiler_params=params(48),
        cost_estimate=pl.CostEstimate(flops=12 << 30, bytes_accessed=24 << 20, transcendentals=1 << 20),
    )(seams, ext, est, mea, above, above_across, above_beside, rim_across, rim_beside, v, l)


def on_device(measured, estimate, extinction, psf_rows, psf_cols, stratum, seam_flags):
    rows = measured.shape[1]
    rim = 2 * HALF
    tiles = lax.axis_size("tile")
    beside = [(i, i ^ 1) for i in range(tiles)]
    across = [p for i in range(1, tiles - 1, 2) for p in ((i, i + 1), (i + 1, i))]
    first_core = lax.axis_index("tile") % 2 == 0
    above, (v, l) = above_of(sums(extinction), bands(psf_rows, psf_cols, stratum))
    send_beside, send_across = rims(extinction, estimate, measured)
    rim_across = lax.ppermute(send_across, "tile", across)
    rim_beside = lax.ppermute(send_beside, "tile", beside)

    def rim_of(at_far):
        return lax.dynamic_slice_in_dim(above, jnp.where(at_far, rows - rim, 0), rim)

    above_across = lax.ppermute(rim_of(~first_core), "tile", across)
    above_beside = lax.ppermute(rim_of(first_core), "tile", beside)
    updated, keep_a, give_a, keep_b, give_b = step(
        seam_flags, extinction, estimate, measured, above, above_across, above_beside, rim_across, rim_beside, v, l
    )
    return updated, highest([(keep_a, give_a), (keep_b, give_b)])


def solution(mesh):
    return jax.shard_map(
        on_device,
        mesh=mesh,
        in_specs=(
            P("depth", "tile", None),
            P("depth", "tile", None),
            P("depth", "tile", None),
            P(),
            P(),
            P("depth"),
            P(),
        ),
        out_specs=(P("depth", "tile", None), P("tile", None)),
        check_vma=False,
    )
```

```python
import jax
import jax.numpy as jnp
from jax import lax
from jax.experimental import pallas as pl
from jax.experimental.pallas import tpu as pltpu
from jax.sharding import PartitionSpec as P

SIDE = 4
HALF = 32
TAPS = 65
BF = jnp.bfloat16
F32 = jnp.float32


def params(mib):
    return pltpu.CompilerParams(vmem_limit_bytes=mib << 20)


def whole():
    return pl.BlockSpec(memory_space=pltpu.VMEM)


def smem():
    return pl.BlockSpec(memory_space=pltpu.SMEM)


PAIRINGS = (
    (("y", 1), ("y", 3), ("x", 1), ("x", 3)),
    (("x", 1), ("x", 3), ("y", 1), ("y", 3)),
)


def pairs(piece, number, tiles):
    result = []
    for x in range(SIDE):
        for y in range(SIDE):
            for tile in range(tiles):
                axis, flip = PAIRINGS[piece][number]
                tx, ty = (x, y ^ flip) if axis == "y" else (x ^ flip, y)
                result.append(((x * SIDE + y) * tiles + tile, (tx * SIDE + ty) * tiles + tile))
    return result


def swap(value, piece, number):
    return lax.ppermute(value, ("depth", "tile"), pairs(piece, number, lax.axis_size("tile")))


def side(piece):
    depth = lax.axis_index("depth")
    axis, _ = PAIRINGS[piece][0]
    value = depth % SIDE if axis == "y" else depth // SIDE
    return (value + 1) // 2 % 2


def split(value):
    high = value.astype(BF)
    return high, (value - high.astype(F32)).astype(BF)


def rows_at(index, size):
    return pl.ds(pl.multiple_of(index * size, size), size)


def sums_kernel(ext, out, buf, sems):
    block = out.shape[0] // sems.shape[0]
    copies = []
    for i in range(sems.shape[0]):
        rows = pl.ds(i * block, block)
        copies.append(pltpu.make_async_copy(ext.at[:, rows], buf.at[:, rows], sems.at[i]))
        copies[-1].start()
    for i, copy in enumerate(copies):
        copy.wait()
        rows = pl.ds(i * block, block)
        total = buf[0, rows]
        for plane in range(1, buf.shape[0]):
            total = total + buf[plane, rows]
        out[rows] = total


def sums(extinction):
    planes, rows, cols = extinction.shape
    return pl.pallas_call(
        sums_kernel,
        in_specs=[pl.BlockSpec(memory_space=pl.ANY)],
        out_specs=whole(),
        out_shape=jax.ShapeDtypeStruct((rows, cols), F32),
        scratch_shapes=[pltpu.VMEM((planes, rows, cols), F32), pltpu.SemaphoreType.DMA((8,))],
        compiler_params=params(60),
    )(extinction)


def rims_kernel(ext, est, mea, beside, across, ext_buf, est_buf, mea_buf, sems):
    rim = 2 * HALF
    planes, rows, _ = ext.shape
    core = lax.axis_index("tile") % 2
    ends = []
    for at_far, out in ((core == 0, beside), (core == 1, across)):
        wide = pl.multiple_of(jnp.where(at_far, rows - rim, 0), HALF)
        narrow = pl.multiple_of(jnp.where(at_far, rows - HALF, 0), HALF)
        ends.append((wide, narrow, out))
    copies = []
    for i, (wide, narrow, _) in enumerate(ends):
        for j, (source, buf, at, size) in enumerate(
            ((ext, ext_buf, wide, rim), (est, est_buf, wide, rim), (mea, mea_buf, narrow, HALF))
        ):
            copies.append(pltpu.make_async_copy(source.at[:, pl.ds(at, size)], buf.at[i], sems.at[3 * i + j]))
            copies[-1].start()
    for i, (_, _, out) in enumerate(ends):
        for copy in copies[3 * i : 3 * i + 3]:
            copy.wait()
        depth = jnp.zeros(ext_buf.shape[2:], F32)
        for plane in range(planes):
            out[plane, :rim] = jnp.exp(-depth) * est_buf[i, plane]
            out[plane, rim:] = mea_buf[i, plane]
            depth = depth + ext_buf[i, plane]


def rims(extinction, estimate, measured):
    planes, rows, cols = extinction.shape
    rim = 2 * HALF
    return pl.pallas_call(
        rims_kernel,
        in_specs=[pl.BlockSpec(memory_space=pl.ANY)] * 3,
        out_specs=[whole()] * 2,
        out_shape=[jax.ShapeDtypeStruct((planes, rim + HALF, cols), F32)] * 2,
        scratch_shapes=[
            pltpu.VMEM((2, planes, rim, cols), F32),
            pltpu.VMEM((2, planes, rim, cols), F32),
            pltpu.VMEM((2, planes, HALF, cols), F32),
            pltpu.SemaphoreType.DMA((6,)),
        ],
        compiler_params=params(60),
        cost_estimate=pl.CostEstimate(flops=1 << 20, bytes_accessed=8 << 20, transcendentals=1 << 19),
    )(extinction, estimate, measured)


def scan_kernel(parts, out):
    running = jnp.zeros(parts.shape[1:], F32)
    for slab in range(parts.shape[0]):
        value = parts[slab]
        out[slab] = running
        running = running + value


def above_of(total, meanwhile, args):
    rows, cols = total.shape
    slabs = lax.axis_size("depth")
    parts = total.reshape(slabs, rows // slabs, cols)
    parts = lax.all_to_all(parts, "depth", 0, 0, tiled=True)
    parts, args = lax.optimization_barrier((parts, args))
    made = meanwhile(*args)
    prefixes = pl.pallas_call(
        scan_kernel,
        in_specs=[whole()],
        out_specs=whole(),
        out_shape=jax.ShapeDtypeStruct(parts.shape, F32),
        compiler_params=params(16),
    )(parts)
    above = lax.all_to_all(prefixes, "depth", 0, 0, tiled=True).reshape(rows, cols)
    return lax.optimization_barrier((above, made))


def highest(parts):
    joined = []
    held = [jnp.maximum(keep, swap(give, piece, 0)) for piece, (keep, give) in enumerate(parts)]
    for number in range(1, 4):
        held = [jnp.maximum(value, swap(value, piece, number)) for piece, value in enumerate(held)]
    for piece, mine in enumerate(held):
        other = swap(mine, piece, 0)
        first = side(piece) == 0
        joined += [jnp.where(first, mine, other), jnp.where(first, other, mine)]
    return jnp.concatenate(joined)


def bands_kernel(stratum, taps, v_ref, l_ref):
    def toeplitz(row, count, shift):
        line = taps[0, row : row + 1]
        line = line / jnp.sum(line, axis=1, keepdims=True)
        wide = jnp.broadcast_to(line, (count, line.shape[1]))
        return pltpu.roll(wide, shift, 1, stride=1, stride_axis=0)

    for way in range(2):
        band = toeplitz(way, v_ref.shape[3], 0)
        v_ref[0, way, 0], v_ref[0, way, 1] = split(band)
        ring = toeplitz(3 - way, 256, 256 - HALF)
        k = lax.broadcasted_iota(jnp.int32, ring.shape, 0)
        n = lax.broadcasted_iota(jnp.int32, ring.shape, 1)
        zero = jnp.zeros_like(ring)
        main = jnp.where(jnp.abs(n - k) <= HALF, ring, zero)
        left = jnp.where(k - n > HALF, ring, zero)[128:]
        right = jnp.where(n - k > HALF, ring, zero)[:128]
        l_ref[0, way, :256], l_ref[0, way, 256:512] = split(main)
        high, low = split(left + right)
        pair = jnp.concatenate([high[:HALF], high[128 - HALF :]], axis=0)
        l_ref[0, way, 512 : 512 + 2 * HALF] = pair
        l_ref[0, way, 512 + 2 * HALF : 640] = pair
        l_ref[0, way, 640:] = low


def bands(psf_rows, psf_cols, stratum):
    planes = stratum.shape[0]
    taps = jnp.stack([psf_rows, psf_rows[:, ::-1], psf_cols, psf_cols[:, ::-1]], axis=1)
    taps = jnp.pad(taps, ((0, 0), (0, 0), (0, 256 - TAPS)))
    return pl.pallas_call(
        bands_kernel,
        grid_spec=pltpu.PrefetchScalarGridSpec(
            num_scalar_prefetch=1,
            grid=(planes,),
            in_specs=[pl.BlockSpec((1, 4, 256), lambda p, s: (s[p], 0, 0))],
            out_specs=[
                pl.BlockSpec((1, 2, 2, 192, 256), lambda p, s: (p, 0, 0, 0, 0)),
                pl.BlockSpec((1, 2, 768, 256), lambda p, s: (p, 0, 0, 0)),
            ],
        ),
        out_shape=[
            jax.ShapeDtypeStruct((planes, 2, 2, 192, 256), BF),
            jax.ShapeDtypeStruct((planes, 2, 768, 256), BF),
        ],
        compiler_params=params(60),
        cost_estimate=pl.CostEstimate(flops=1 << 22, bytes_accessed=6 << 20, transcendentals=0),
    )(stratum, taps)


def dot(a, b):
    return jnp.dot(a, b, preferred_element_type=F32)


def corners(high, low, out):
    for c in range(0, out.shape[1], 256):
        left, right = slice(c, c + 128), slice(c + 384, c + 512)
        for r in range(0, out.shape[0], 64):
            t = slice(r, r + 64)
            lane = lax.broadcasted_iota(jnp.int32, (64, 128), 1)
            near = lane < 64
            h = jnp.where(near, high[t, right].astype(F32), high[t, left].astype(F32))
            w = jnp.where(near, low[t, right].astype(F32), low[t, left].astype(F32))
            between = (lane >= HALF) & (lane < 128 - HALF)
            out[t, c : c + 128] = jnp.where(between, pltpu.roll(w, 64, 1), h).astype(BF)
            out[t, c + 128 : c + 256] = h.astype(BF)


def lateral(high, low, corner, rows, c, band):
    s = slice(c + 128, c + 384)
    source = jnp.concatenate(
        [high[rows, s], high[rows, s], low[rows, s], corner[rows, c : c + 256]], axis=1
    )
    weights = jnp.concatenate([band[:512], band[:256], band[512:]], axis=0)
    return dot(source, weights)


def step_kernel(
    seams, ext, est, mea, above, above_across, above_beside, rim_across, rim_beside, v_ref, l_ref,
    upd, o0, o1, o2, o3, optical, top, wh, wl, mh, ml, qh, ql, nh, nl, corner,
):
    plane = pl.program_id(0)
    tile = lax.axis_index("tile")
    rows, cols = optical.shape
    rim = 2 * HALF
    ends = lax.axis_size("tile") - 1
    join_top = jnp.where(tile > 0, seams[jnp.maximum(tile - 1, 0)], 0) == 1
    join_bot = jnp.where(tile < ends, seams[jnp.minimum(tile, ends - 1)], 0) == 1

    @pl.when(plane == 0)
    def _():
        optical[...] = above[...]
        for ref in (mh, ml, nh, nl):
            edge = jnp.zeros((ref.shape[0], 128), BF)
            ref[:, :128] = edge
            ref[:, ref.shape[1] - 128 :] = edge

    core = tile % 2

    def top_of(across, beside):
        return jnp.where(core == 0, across, beside)

    def bot_of(across, beside):
        return jnp.where(core == 0, beside, across)

    for joined, pick, at in ((join_top, top_of, 0), (join_bot, bot_of, rows + rim)):
        far = pick(above_across[...], above_beside[...])
        packed = pick(rim_across[0, :rim], rim_beside[0, :rim])
        value = jnp.where(joined, jnp.exp(-far) * packed, 0.0)
        wh[at : at + rim], wl[at : at + rim] = split(value)
    for r in range(0, rows, 64):
        depth = optical[r : r + 64]
        value = jnp.exp(-depth) * est[0, r : r + 64]
        wh[rim + r : rim + r + 64], wl[rim + r : rim + r + 64] = split(value)
        optical[r : r + 64] = depth + ext[0, r : r + 64]

    def vertical(way, sh, sl, dh, dl):
        total = dh.shape[0]
        for at in range(0, total, 192):
            m = min(192, total - at)
            depth = min(256, m + rim)
            th, tl = v_ref[0, way, 0, :m, :depth], v_ref[0, way, 1, :m, :depth]
            for c in range(0, cols, 256):
                both = dot(jnp.concatenate([th, tl], axis=0), sh[at : at + depth, c : c + 256])
                result = both[:m] + (both[m:] + dot(th, sl[at : at + depth, c : c + 256]))
                dh[at : at + m, 128 + c : 384 + c], dl[at : at + m, 128 + c : 384 + c] = split(result)

    vertical(0, wh, wl, mh, ml)
    corners(mh, ml, corner)
    for c in range(0, cols, 256):
        s = slice(c, c + 256)
        blurred = lateral(mh, ml, corner, slice(0, rows + rim), c, l_ref.at[0, 0])
        q0 = top_of(rim_across[0, rim:, s], rim_beside[0, rim:, s]) / blurred[:HALF]
        q0 = jnp.where(join_top, q0, 0.0)
        q1 = mea[0, :, s] / blurred[HALF : HALF + rows]
        q2 = bot_of(rim_across[0, rim:, s], rim_beside[0, rim:, s]) / blurred[HALF + rows :]
        q2 = jnp.where(join_bot, q2, 0.0)
        qh[:HALF, s], ql[:HALF, s] = split(q0)
        qh[HALF : HALF + rows, s], ql[HALF : HALF + rows, s] = split(q1)
        qh[HALF + rows :, s], ql[HALF + rows :, s] = split(q2)

    vertical(1, qh, ql, nh, nl)
    ours = corner.at[pl.ds(0, rows)]
    corners(nh, nl, ours)
    for c in range(0, cols, 256):
        s = slice(c, c + 256)
        result = est[0, :, s] * lateral(nh, nl, ours, slice(0, rows), c, l_ref.at[0, 1])
        upd[0, :, s] = result
        top[:, s] = jnp.maximum(jnp.where(plane == 0, result, top[:, s]), result)

    @pl.when(plane == pl.num_programs(0) - 1)
    def _():
        quarter = rows // 4
        for piece, (keep, give) in enumerate(((o0, o1), (o2, o3))):
            kept = side(piece)
            keep[...] = top[rows_at(2 * piece + kept, quarter)]
            give[...] = top[rows_at(2 * piece + 1 - kept, quarter)]


def step(seams, ext, est, mea, above, above_across, above_beside, rim_across, rim_beside, v, l):
    planes, rows, cols = ext.shape
    rim, quarter = 2 * HALF, rows // 4
    stack = pl.BlockSpec((1, rows, cols), lambda p: (p, 0, 0))
    pack = pl.BlockSpec((1, rim + HALF, cols), lambda p: (p, 0, 0))
    part = pl.BlockSpec((quarter, cols), lambda p: (0, 0))
    return pl.pallas_call(
        step_kernel,
        grid=(planes,),
        in_specs=[
            smem(), stack, stack, stack, whole(), whole(), whole(), pack, pack,
            pl.BlockSpec((1,) + v.shape[1:], lambda p: (p, 0, 0, 0, 0)),
            pl.BlockSpec((1,) + l.shape[1:], lambda p: (p, 0, 0, 0)),
        ],
        out_specs=[stack] + [part] * 4,
        out_shape=[jax.ShapeDtypeStruct((planes, rows, cols), F32)]
        + [jax.ShapeDtypeStruct((quarter, cols), F32)] * 4,
        scratch_shapes=[
            pltpu.VMEM((rows, cols), F32),
            pltpu.VMEM((rows, cols), F32),
            pltpu.VMEM((rows + 2 * rim, cols), BF),
            pltpu.VMEM((rows + 2 * rim, cols), BF),
            pltpu.VMEM((rows + rim, cols + 256), BF),
            pltpu.VMEM((rows + rim, cols + 256), BF),
            pltpu.VMEM((rows + rim, cols), BF),
            pltpu.VMEM((rows + rim, cols), BF),
            pltpu.VMEM((rows, cols + 256), BF),
            pltpu.VMEM((rows, cols + 256), BF),
            pltpu.VMEM((rows + rim, cols), BF),
        ],
        compiler_params=params(48),
        cost_estimate=pl.CostEstimate(flops=12 << 30, bytes_accessed=24 << 20, transcendentals=1 << 20),
    )(seams, ext, est, mea, above, above_across, above_beside, rim_across, rim_beside, v, l)


def on_device(measured, estimate, extinction, psf_rows, psf_cols, stratum, seam_flags):
    rows = measured.shape[1]
    rim = 2 * HALF
    tiles = lax.axis_size("tile")
    beside = [(i, i ^ 1) for i in range(tiles)]
    across = [p for i in range(1, tiles - 1, 2) for p in ((i, i + 1), (i + 1, i))]
    first_core = lax.axis_index("tile") % 2 == 0
    above, (v, l) = above_of(sums(extinction), bands, (psf_rows, psf_cols, stratum))
    send_beside, send_across = rims(extinction, estimate, measured)
    rim_across = lax.ppermute(send_across, "tile", across)
    rim_beside = lax.ppermute(send_beside, "tile", beside)

    def rim_of(at_far):
        return lax.dynamic_slice_in_dim(above, jnp.where(at_far, rows - rim, 0), rim)

    above_across = lax.ppermute(rim_of(~first_core), "tile", across)
    above_beside = lax.ppermute(rim_of(first_core), "tile", beside)
    updated, keep_a, give_a, keep_b, give_b = step(
        seam_flags, extinction, estimate, measured, above, above_across, above_beside, rim_across, rim_beside, v, l
    )
    return updated, highest([(keep_a, give_a), (keep_b, give_b)])


def solution(mesh):
    return jax.shard_map(
        on_device,
        mesh=mesh,
        in_specs=(
            P("depth", "tile", None),
            P("depth", "tile", None),
            P("depth", "tile", None),
            P(),
            P(),
            P("depth"),
            P(),
        ),
        out_specs=(P("depth", "tile", None), P("tile", None)),
        check_vma=False,
    )
```

```python
import jax
import jax.numpy as jnp
from jax import lax
from jax.experimental import pallas as pl
from jax.experimental.pallas import tpu as pltpu
from jax.sharding import PartitionSpec as P

SIDE = 4
HALF = 32
TAPS = 65
BF = jnp.bfloat16
F32 = jnp.float32


def params(mib):
    return pltpu.CompilerParams(vmem_limit_bytes=mib << 20)


def whole():
    return pl.BlockSpec(memory_space=pltpu.VMEM)


def smem():
    return pl.BlockSpec(memory_space=pltpu.SMEM)


def first_place():
    depth = lax.axis_index("depth")
    return jnp.where(lax.axis_index("tile") % 2 == 0, depth % SIDE, depth // SIDE)


def shifts(stage, k, tiles):
    result = []
    for x in range(SIDE):
        for y in range(SIDE):
            for tile in range(tiles):
                along_y = (tile % 2 == 0) == (stage == 0)
                tx, ty = (x, (y + k) % SIDE) if along_y else ((x + k) % SIDE, y)
                result.append(((x * SIDE + y) * tiles + tile, (tx * SIDE + ty) * tiles + tile))
    return result


def around(stage, parts):
    tiles = lax.axis_size("tile")
    got = [parts[0]] + [None] * (SIDE - 1)
    for k in (2, 1, 3):
        got[k] = lax.ppermute(parts[k], ("depth", "tile"), shifts(stage, k, tiles))
    return got


def split(value):
    high = value.astype(BF)
    return high, (value - high.astype(F32)).astype(BF)


def rows_at(index, size):
    return pl.ds(pl.multiple_of(index * size, size), size)


def sums_kernel(ext, out, buf, sems):
    block = out.shape[0] // sems.shape[0]
    copies = []
    for i in range(sems.shape[0]):
        rows = pl.ds(i * block, block)
        copies.append(pltpu.make_async_copy(ext.at[:, rows], buf.at[:, rows], sems.at[i]))
        copies[-1].start()
    for i, copy in enumerate(copies):
        copy.wait()
        rows = pl.ds(i * block, block)
        total = buf[0, rows]
        for plane in range(1, buf.shape[0]):
            total = total + buf[plane, rows]
        out[rows] = total


def sums(extinction):
    planes, rows, cols = extinction.shape
    return pl.pallas_call(
        sums_kernel,
        in_specs=[pl.BlockSpec(memory_space=pl.ANY)],
        out_specs=whole(),
        out_shape=jax.ShapeDtypeStruct((rows, cols), F32),
        scratch_shapes=[pltpu.VMEM((planes, rows, cols), F32), pltpu.SemaphoreType.DMA((8,))],
        compiler_params=params(60),
    )(extinction)


def rims_kernel(ext, est, mea, beside, across, ext_buf, est_buf, mea_buf, sems):
    rim = 2 * HALF
    planes, rows, _ = ext.shape
    core = lax.axis_index("tile") % 2
    ends = []
    for at_far, out in ((core == 0, beside), (core == 1, across)):
        wide = pl.multiple_of(jnp.where(at_far, rows - rim, 0), HALF)
        narrow = pl.multiple_of(jnp.where(at_far, rows - HALF, 0), HALF)
        ends.append((wide, narrow, out))
    copies = []
    for i, (wide, narrow, _) in enumerate(ends):
        for j, (source, buf, at, size) in enumerate(
            ((ext, ext_buf, wide, rim), (est, est_buf, wide, rim), (mea, mea_buf, narrow, HALF))
        ):
            copies.append(pltpu.make_async_copy(source.at[:, pl.ds(at, size)], buf.at[i], sems.at[3 * i + j]))
            copies[-1].start()
    for i, (_, _, out) in enumerate(ends):
        for copy in copies[3 * i : 3 * i + 3]:
            copy.wait()
        depth = jnp.zeros(ext_buf.shape[2:], F32)
        for plane in range(planes):
            out[plane, :rim] = jnp.exp(-depth) * est_buf[i, plane]
            out[plane, rim:] = mea_buf[i, plane]
            depth = depth + ext_buf[i, plane]


def rims(extinction, estimate, measured):
    planes, rows, cols = extinction.shape
    rim = 2 * HALF
    return pl.pallas_call(
        rims_kernel,
        in_specs=[pl.BlockSpec(memory_space=pl.ANY)] * 3,
        out_specs=[whole()] * 2,
        out_shape=[jax.ShapeDtypeStruct((planes, rim + HALF, cols), F32)] * 2,
        scratch_shapes=[
            pltpu.VMEM((2, planes, rim, cols), F32),
            pltpu.VMEM((2, planes, rim, cols), F32),
            pltpu.VMEM((2, planes, HALF, cols), F32),
            pltpu.SemaphoreType.DMA((6,)),
        ],
        compiler_params=params(60),
        cost_estimate=pl.CostEstimate(flops=1 << 20, bytes_accessed=8 << 20, transcendentals=1 << 19),
    )(extinction, estimate, measured)


def scan_kernel(parts, out):
    running = jnp.zeros(parts.shape[1:], F32)
    for slab in range(parts.shape[0]):
        value = parts[slab]
        out[slab] = running
        running = running + value


def above_of(total, meanwhile, args):
    rows, cols = total.shape
    slabs = lax.axis_size("depth")
    parts = total.reshape(slabs, rows // slabs, cols)
    parts = lax.all_to_all(parts, "depth", 0, 0, tiled=True)
    parts, args = lax.optimization_barrier((parts, args))
    made = meanwhile(*args)
    prefixes = pl.pallas_call(
        scan_kernel,
        in_specs=[whole()],
        out_specs=whole(),
        out_shape=jax.ShapeDtypeStruct(parts.shape, F32),
        compiler_params=params(16),
    )(parts)
    above = lax.all_to_all(prefixes, "depth", 0, 0, tiled=True).reshape(rows, cols)
    return lax.optimization_barrier((above, made))


def top_of_four(parts):
    return jnp.maximum(jnp.maximum(parts[0], parts[1]), jnp.maximum(parts[2], parts[3]))


def highest(parts):
    mine = top_of_four(around(0, parts))
    mine = top_of_four(around(1, [mine] * SIDE))
    got = around(0, [mine] * SIDE)
    first = first_place()
    quarters = []
    for j in range(SIDE):
        back = (first - j + SIDE) % SIDE
        near = jnp.where(back == 0, got[0], got[1])
        quarters.append(jnp.where(back < 2, near, jnp.where(back == 2, got[2], got[3])))
    return jnp.concatenate(quarters)


def bands_kernel(stratum, taps, v_ref, l_ref):
    def toeplitz(row, count, shift):
        line = taps[0, row : row + 1]
        line = line / jnp.sum(line, axis=1, keepdims=True)
        wide = jnp.broadcast_to(line, (count, line.shape[1]))
        return pltpu.roll(wide, shift, 1, stride=1, stride_axis=0)

    for way in range(2):
        band = toeplitz(way, v_ref.shape[3], 0)
        v_ref[0, way, 0], v_ref[0, way, 1] = split(band)
        ring = toeplitz(3 - way, 256, 256 - HALF)
        k = lax.broadcasted_iota(jnp.int32, ring.shape, 0)
        n = lax.broadcasted_iota(jnp.int32, ring.shape, 1)
        zero = jnp.zeros_like(ring)
        main = jnp.where(jnp.abs(n - k) <= HALF, ring, zero)
        left = jnp.where(k - n > HALF, ring, zero)[128:]
        right = jnp.where(n - k > HALF, ring, zero)[:128]
        l_ref[0, way, :256], l_ref[0, way, 256:512] = split(main)
        high, low = split(left + right)
        pair = jnp.concatenate([high[:HALF], high[128 - HALF :]], axis=0)
        l_ref[0, way, 512 : 512 + 2 * HALF] = pair
        l_ref[0, way, 512 + 2 * HALF : 640] = pair
        l_ref[0, way, 640:] = low


def bands(psf_rows, psf_cols, stratum):
    planes = stratum.shape[0]
    taps = jnp.stack([psf_rows, psf_rows[:, ::-1], psf_cols, psf_cols[:, ::-1]], axis=1)
    taps = jnp.pad(taps, ((0, 0), (0, 0), (0, 256 - TAPS)))
    return pl.pallas_call(
        bands_kernel,
        grid_spec=pltpu.PrefetchScalarGridSpec(
            num_scalar_prefetch=1,
            grid=(planes,),
            in_specs=[pl.BlockSpec((1, 4, 256), lambda p, s: (s[p], 0, 0))],
            out_specs=[
                pl.BlockSpec((1, 2, 2, 192, 256), lambda p, s: (p, 0, 0, 0, 0)),
                pl.BlockSpec((1, 2, 768, 256), lambda p, s: (p, 0, 0, 0)),
            ],
        ),
        out_shape=[
            jax.ShapeDtypeStruct((planes, 2, 2, 192, 256), BF),
            jax.ShapeDtypeStruct((planes, 2, 768, 256), BF),
        ],
        compiler_params=params(60),
        cost_estimate=pl.CostEstimate(flops=1 << 22, bytes_accessed=6 << 20, transcendentals=0),
    )(stratum, taps)


def dot(a, b):
    return jnp.dot(a, b, preferred_element_type=F32)


def corners(high, low, out):
    for c in range(0, out.shape[1], 256):
        left, right = slice(c, c + 128), slice(c + 384, c + 512)
        for r in range(0, out.shape[0], 64):
            t = slice(r, r + 64)
            lane = lax.broadcasted_iota(jnp.int32, (64, 128), 1)
            near = lane < 64
            h = jnp.where(near, high[t, right].astype(F32), high[t, left].astype(F32))
            w = jnp.where(near, low[t, right].astype(F32), low[t, left].astype(F32))
            between = (lane >= HALF) & (lane < 128 - HALF)
            out[t, c : c + 128] = jnp.where(between, pltpu.roll(w, 64, 1), h).astype(BF)
            out[t, c + 128 : c + 256] = h.astype(BF)


def lateral(high, low, corner, rows, c, band):
    s = slice(c + 128, c + 384)
    source = jnp.concatenate(
        [high[rows, s], high[rows, s], low[rows, s], corner[rows, c : c + 256]], axis=1
    )
    weights = jnp.concatenate([band[:512], band[:256], band[512:]], axis=0)
    return dot(source, weights)


def step_kernel(
    seams, ext, est, mea, above, above_across, above_beside, rim_across, rim_beside, v_ref, l_ref,
    upd, o0, o1, o2, o3, optical, top, wh, wl, mh, ml, qh, ql, nh, nl, corner,
):
    plane = pl.program_id(0)
    tile = lax.axis_index("tile")
    rows, cols = optical.shape
    rim = 2 * HALF
    ends = lax.axis_size("tile") - 1
    join_top = jnp.where(tile > 0, seams[jnp.maximum(tile - 1, 0)], 0) == 1
    join_bot = jnp.where(tile < ends, seams[jnp.minimum(tile, ends - 1)], 0) == 1

    @pl.when(plane == 0)
    def _():
        optical[...] = above[...]
        for ref in (mh, ml, nh, nl):
            edge = jnp.zeros((ref.shape[0], 128), BF)
            ref[:, :128] = edge
            ref[:, ref.shape[1] - 128 :] = edge

    core = tile % 2

    def top_of(across, beside):
        return jnp.where(core == 0, across, beside)

    def bot_of(across, beside):
        return jnp.where(core == 0, beside, across)

    for joined, pick, at in ((join_top, top_of, 0), (join_bot, bot_of, rows + rim)):
        far = pick(above_across[...], above_beside[...])
        packed = pick(rim_across[0, :rim], rim_beside[0, :rim])
        value = jnp.where(joined, jnp.exp(-far) * packed, 0.0)
        wh[at : at + rim], wl[at : at + rim] = split(value)
    for r in range(0, rows, 64):
        depth = optical[r : r + 64]
        value = jnp.exp(-depth) * est[0, r : r + 64]
        wh[rim + r : rim + r + 64], wl[rim + r : rim + r + 64] = split(value)
        optical[r : r + 64] = depth + ext[0, r : r + 64]

    def vertical(way, sh, sl, dh, dl):
        total = dh.shape[0]
        for at in range(0, total, 192):
            m = min(192, total - at)
            depth = min(256, m + rim)
            th, tl = v_ref[0, way, 0, :m, :depth], v_ref[0, way, 1, :m, :depth]
            for c in range(0, cols, 256):
                both = dot(jnp.concatenate([th, tl], axis=0), sh[at : at + depth, c : c + 256])
                result = both[:m] + (both[m:] + dot(th, sl[at : at + depth, c : c + 256]))
                dh[at : at + m, 128 + c : 384 + c], dl[at : at + m, 128 + c : 384 + c] = split(result)

    vertical(0, wh, wl, mh, ml)
    corners(mh, ml, corner)
    for c in range(0, cols, 256):
        s = slice(c, c + 256)
        blurred = lateral(mh, ml, corner, slice(0, rows + rim), c, l_ref.at[0, 0])
        q0 = top_of(rim_across[0, rim:, s], rim_beside[0, rim:, s]) / blurred[:HALF]
        q0 = jnp.where(join_top, q0, 0.0)
        q1 = mea[0, :, s] / blurred[HALF : HALF + rows]
        q2 = bot_of(rim_across[0, rim:, s], rim_beside[0, rim:, s]) / blurred[HALF + rows :]
        q2 = jnp.where(join_bot, q2, 0.0)
        qh[:HALF, s], ql[:HALF, s] = split(q0)
        qh[HALF : HALF + rows, s], ql[HALF : HALF + rows, s] = split(q1)
        qh[HALF + rows :, s], ql[HALF + rows :, s] = split(q2)

    vertical(1, qh, ql, nh, nl)
    ours = corner.at[pl.ds(0, rows)]
    corners(nh, nl, ours)
    for c in range(0, cols, 256):
        s = slice(c, c + 256)
        result = est[0, :, s] * lateral(nh, nl, ours, slice(0, rows), c, l_ref.at[0, 1])
        upd[0, :, s] = result
        top[:, s] = jnp.maximum(jnp.where(plane == 0, result, top[:, s]), result)

    @pl.when(plane == pl.num_programs(0) - 1)
    def _():
        for k, out in enumerate((o0, o1, o2, o3)):
            out[...] = top[rows_at(lax.rem(first_place() + k, SIDE), rows // SIDE)]


def step(seams, ext, est, mea, above, above_across, above_beside, rim_across, rim_beside, v, l):
    planes, rows, cols = ext.shape
    rim, quarter = 2 * HALF, rows // 4
    stack = pl.BlockSpec((1, rows, cols), lambda p: (p, 0, 0))
    pack = pl.BlockSpec((1, rim + HALF, cols), lambda p: (p, 0, 0))
    part = pl.BlockSpec((quarter, cols), lambda p: (0, 0))
    return pl.pallas_call(
        step_kernel,
        grid=(planes,),
        in_specs=[
            smem(), stack, stack, stack, whole(), whole(), whole(), pack, pack,
            pl.BlockSpec((1,) + v.shape[1:], lambda p: (p, 0, 0, 0, 0)),
            pl.BlockSpec((1,) + l.shape[1:], lambda p: (p, 0, 0, 0)),
        ],
        out_specs=[stack] + [part] * 4,
        out_shape=[jax.ShapeDtypeStruct((planes, rows, cols), F32)]
        + [jax.ShapeDtypeStruct((quarter, cols), F32)] * 4,
        scratch_shapes=[
            pltpu.VMEM((rows, cols), F32),
            pltpu.VMEM((rows, cols), F32),
            pltpu.VMEM((rows + 2 * rim, cols), BF),
            pltpu.VMEM((rows + 2 * rim, cols), BF),
            pltpu.VMEM((rows + rim, cols + 256), BF),
            pltpu.VMEM((rows + rim, cols + 256), BF),
            pltpu.VMEM((rows + rim, cols), BF),
            pltpu.VMEM((rows + rim, cols), BF),
            pltpu.VMEM((rows, cols + 256), BF),
            pltpu.VMEM((rows, cols + 256), BF),
            pltpu.VMEM((rows + rim, cols), BF),
        ],
        compiler_params=params(48),
        cost_estimate=pl.CostEstimate(flops=12 << 30, bytes_accessed=24 << 20, transcendentals=1 << 20),
    )(seams, ext, est, mea, above, above_across, above_beside, rim_across, rim_beside, v, l)


def on_device(measured, estimate, extinction, psf_rows, psf_cols, stratum, seam_flags):
    rows = measured.shape[1]
    rim = 2 * HALF
    tiles = lax.axis_size("tile")
    beside = [(i, i ^ 1) for i in range(tiles)]
    across = [p for i in range(1, tiles - 1, 2) for p in ((i, i + 1), (i + 1, i))]
    first_core = lax.axis_index("tile") % 2 == 0
    above, (v, l) = above_of(sums(extinction), bands, (psf_rows, psf_cols, stratum))
    send_beside, send_across = rims(extinction, estimate, measured)
    rim_across = lax.ppermute(send_across, "tile", across)
    rim_beside = lax.ppermute(send_beside, "tile", beside)

    def rim_of(at_far):
        return lax.dynamic_slice_in_dim(above, jnp.where(at_far, rows - rim, 0), rim)

    above_across = lax.ppermute(rim_of(~first_core), "tile", across)
    above_beside = lax.ppermute(rim_of(first_core), "tile", beside)
    updated, *tops = step(
        seam_flags, extinction, estimate, measured, above, above_across, above_beside, rim_across, rim_beside, v, l
    )
    return updated, highest(tops)


def solution(mesh):
    return jax.shard_map(
        on_device,
        mesh=mesh,
        in_specs=(
            P("depth", "tile", None),
            P("depth", "tile", None),
            P("depth", "tile", None),
            P(),
            P(),
            P("depth"),
            P(),
        ),
        out_specs=(P("depth", "tile", None), P("tile", None)),
        check_vma=False,
    )
```
